32 devices in a mesh: leaf: 8 (over z, y), top: 4 (over x, core).
Axes of the slice: x: 2, y: 2, z: 4, core: 2. Of those that a mesh axis runs over, the one named last changes fastest.
Arguments:
- coords: float32 [4, 8, 8, 4096], P('top', 'leaf'), may hold values from 0 to 1
- order: int32 [4, 8, 4096], P('top', 'leaf'), may hold values from 0 to 4095, each once within a row
- charges: bfloat16 [4, 8, 64, 4096], P('top', 'leaf'), may hold values from -6 to 6
- leaf_basis: bfloat16 [4, 8, 4, 128, 1024], P('top', 'leaf'), may hold values from -0.1875 to 0.1875
- leaf_factors: bfloat16 [4, 8, 4, 2, 2, 128, 128], P('top', 'leaf'), may hold values from -0.5 to 0.5
- transfer: bfloat16 [4, 8, 4, 128, 128], P('top', 'leaf'), may hold values from -0.5 to 0.5
- block_factors: bfloat16 [4, 8, 5, 2, 128, 128], P('top', 'leaf'), may hold values from -0.5 to 0.5
Outputs:
- potential: bfloat16 [4, 8, 64, 4096], P('top', 'leaf')
The draws below stay inside these ranges and needn't reach their ends.
Inputs may be any that keep to these rules, and one draw needn't show every extreme that they name: Each block's row of order holds every number 0 to 4095 once.
All inputs are finite; a program needn't handle non-finite values.
Results may differ from the reference program's by a relative error of at most 0.0047.
Values sent between devices are 32-bit elements; how exact they have to be, the bound alone decides.
A program may use at most 64 MiB of HBM per device.

```python
import jax
import jax.numpy as jnp
from jax import lax

DIM = 8
LEAF = 1024
RANK = 128
RHS = 64
LEAF_DEV = 4
PTS = 4096
GROUPS = 4
BLOCKS = 8
LOCAL_BITS = 2
CROSS_BITS = 5


def steps_of(stream_key, extent, split, low, high):
    factor_of, own = 1.0, jax.random.fold_in(stream_key, 6)
    for position, shards_of in split:
        heights = jnp.exp(jax.random.uniform(jax.random.fold_in(own, position), (shards_of,), jnp.float32, low / len(split), high / len(split)))
        factor_of = factor_of * jnp.repeat(heights, extent[position] // shards_of).reshape([-1 if axis == position else 1 for axis in range(len(extent))])
    return factor_of


def noise(key, shape, scale, reach, shards=(), kind=jnp.bfloat16):
    values = jax.random.normal(key, shape, jnp.float32) * scale
    if len(shards) > 0:
        values = steps_of(key, shape, shards, -0.22, 0.18) * values
    return jnp.clip(values, min=-reach, max=reach).astype(kind)


def setup_inputs(seed: int = 0) -> dict:
    seeds = jax.random.split(jax.random.key(seed), 8)
    coords = jnp.clip(1.0 * jax.random.uniform(seeds[0], (GROUPS, BLOCKS, DIM, PTS), jnp.float32) ** steps_of(seeds[0], (GROUPS, BLOCKS, DIM, PTS), ((0, 4), (1, 8)), -0.2, 0.2), 0.0, 1.0)
    order = jax.vmap(lambda own: jax.random.permutation(own, PTS))(jax.random.split(seeds[1], GROUPS * BLOCKS)).reshape((GROUPS, BLOCKS, PTS)).astype(jnp.int32)
    charges = noise(seeds[2], (GROUPS, BLOCKS, RHS, PTS), 1.0, 6.0, ((0, 4), (1, 8)))
    leaf_basis = noise(seeds[3], (GROUPS, BLOCKS, LEAF_DEV, RANK, LEAF), LEAF ** -0.5, 0.1875, ((0, 4), (1, 8)))
    leaf_factors = noise(seeds[4], (GROUPS, BLOCKS, LEAF_DEV, LOCAL_BITS, 2, RANK, RANK), RANK ** -0.5, 0.5, ((0, 4), (1, 8)))
    transfer = noise(seeds[5], (GROUPS, BLOCKS, LEAF_DEV, RANK, RANK), RANK ** -0.5, 0.5, ((0, 4), (1, 8)))
    block_factors = noise(seeds[6], (GROUPS, BLOCKS, CROSS_BITS, 2, RANK, RANK), RANK ** -0.5, 0.5, ((0, 4), (1, 8)))
    return {"coords": coords, "order": order, "charges": charges, "leaf_basis": leaf_basis, "leaf_factors": leaf_factors, "transfer": transfer, "block_factors": block_factors}


kernel_rate = 4.0
highest = lax.Precision.HIGHEST


def kernel_block(points):
    sq_norms = jnp.sum(points * points, axis=0)
    inner_prod = lax.dot_general(points, points, (((0,), (0,)), ((), ())), precision=highest, preferred_element_type=jnp.float32)
    return jnp.exp(-kernel_rate * (sq_norms[:, None] + sq_norms[None, :] - 2.0 * inner_prod)).astype(jnp.bfloat16)


def near_leaf(pair_in):
    points, leaf_vals = pair_in
    kernel = kernel_block(points)
    return lax.dot_general(leaf_vals.astype(jnp.float32), kernel.astype(jnp.float32), (((1,), (1,)), ((), ())), precision=highest, preferred_element_type=jnp.float32)


def sibling_total(partial_value, height):
    nodes_len = partial_value.shape[0]
    subtree = 2 ** height
    grouped = partial_value.reshape((nodes_len // (2 * subtree), 2, subtree) + partial_value.shape[1:]).sum(axis=2)
    swapped = jnp.flip(grouped, axis=1)
    spread = jnp.broadcast_to(swapped[:, :, None], (nodes_len // (2 * subtree), 2, subtree) + partial_value.shape[1:])
    return spread.reshape(partial_value.shape) * (0.5 ** (height / 2.0))


def local_terms(tree_vals, basis, factors, transfer):
    leaves = basis.shape[0]
    leaf_len = basis.shape[2]
    by_leaf = tree_vals.reshape(tree_vals.shape[0], leaves, leaf_len).astype(jnp.float32)
    skeleton = jnp.einsum('rjn,jkn->jrk', by_leaf, basis.astype(jnp.float32), precision=highest)
    right_gen = factors[:, :, 0].astype(jnp.float32)
    left_gen = factors[:, :, 1].astype(jnp.float32)
    leaf_terms = jnp.einsum('jrk,jhkl->jhrl', skeleton, right_gen, precision=highest)
    coeffs = jnp.zeros(skeleton.shape, jnp.float32)
    for height in range(leaf_terms.shape[1]):
        summed = sibling_total(leaf_terms[:, height], height)
        coeffs = coeffs + jnp.einsum('jrk,jkl->jrl', summed, left_gen[:, height], precision=highest)
    block_sum = jnp.einsum('jrk,jkl->rl', skeleton, transfer.astype(jnp.float32), precision=highest)
    return coeffs, block_sum


def finish_block(perm_idx, values, points, basis, transfer, local_coeffs, block_coeffs):
    leaves = basis.shape[0]
    leaf_len = basis.shape[2]
    rhs_len = values.shape[0]
    tree_vals = values[:, perm_idx]
    tree_pts = points[:, perm_idx]
    leaf_vals = tree_vals.reshape(rhs_len, leaves, leaf_len).transpose(1, 0, 2)
    leaf_coords = tree_pts.reshape(points.shape[0], leaves, leaf_len).transpose(1, 0, 2)
    near = lax.map(near_leaf, (leaf_coords, leaf_vals))
    coeffs = local_coeffs + jnp.einsum('rl,jkl->jrk', block_coeffs, transfer.astype(jnp.float32), precision=highest)
    coeffs = coeffs.astype(jnp.bfloat16)
    far = jnp.einsum('jrk,jkn->jrn', coeffs.astype(jnp.float32), basis.astype(jnp.float32), precision=highest)
    field = (near + far).transpose(1, 0, 2).reshape(rhs_len, leaves * leaf_len).astype(jnp.bfloat16)
    return jnp.zeros((rhs_len, leaves * leaf_len), jnp.bfloat16).at[:, perm_idx].set(field)


def reference(coords, order, charges, leaf_basis, leaf_factors, transfer, block_factors):
    n_blocks = order.shape[0] * order.shape[1]
    perm_all = order.reshape(n_blocks, order.shape[2])
    values_all = charges.reshape((n_blocks,) + charges.shape[2:])
    coords_all = coords.reshape((n_blocks,) + coords.shape[2:])
    basis_all = leaf_basis.reshape((n_blocks,) + leaf_basis.shape[2:])
    factors_all = leaf_factors.reshape((n_blocks,) + leaf_factors.shape[2:])
    transfer_all = transfer.reshape((n_blocks,) + transfer.shape[2:])
    cross_all = block_factors.reshape((n_blocks,) + block_factors.shape[2:]).astype(jnp.float32)

    def section_one(pair_in):
        perm_idx, values, basis, factors, trans_mat = pair_in
        return local_terms(values[:, perm_idx], basis, factors, trans_mat)

    local_all, block_sums = lax.map(section_one, (perm_all, values_all, basis_all, factors_all, transfer_all))
    cross_terms = jnp.einsum('brk,bhkl->bhrl', block_sums, cross_all[:, :, 0], precision=highest)
    block_coeffs = jnp.zeros(block_sums.shape, jnp.float32)
    for height in range(cross_terms.shape[1]):
        summed = sibling_total(cross_terms[:, height], height)
        block_coeffs = block_coeffs + jnp.einsum('brk,bkl->brl', summed, cross_all[:, height, 1], precision=highest)

    def section_two(pair_in):
        perm_idx, values, points, basis, trans_mat, own_coeffs, dev_coeffs = pair_in
        return finish_block(perm_idx, values, points, basis, trans_mat, own_coeffs, dev_coeffs)

    result = lax.map(section_two, (perm_all, values_all, coords_all, basis_all, transfer_all, local_all, block_coeffs))
    return result.reshape(charges.shape)
```

```python
import functools

import jax
import jax.numpy as jnp
from jax import lax
from jax.experimental import pallas as pl
from jax.experimental.pallas import tpu as pltpu
from jax.sharding import PartitionSpec as P

kernel_rate = 4.0
WIDTH = 128
UNROLL = 32
ROWS = 256
MESH = pl.DeviceIdType.MESH
VMEM = pl.BlockSpec(memory_space=pltpu.VMEM)
SMEM = pl.BlockSpec(memory_space=pltpu.SMEM)
f32, bf16 = jnp.float32, jnp.bfloat16


def split3(x):
    hi = x.astype(bf16).astype(f32)
    mid = (x - hi).astype(bf16).astype(f32)
    lo = (x - hi - mid).astype(bf16).astype(f32)
    return hi, mid, lo


def dot(a, b, dims=((1,), (0,))):
    return lax.dot_general(a, b, (dims, ((), ())), preferred_element_type=f32)


def dot_split(x, w):
    hi = x.astype(bf16)
    lo = (x - hi.astype(f32)).astype(bf16)
    return dot(hi, w) + dot(lo, w)


def up_kernel(order, coords, charges, basis, transfer, factors, rows_out, skel_out, terms_out, src, dst):
    rhs, points = charges.shape
    dim = coords.shape[0]
    leaves, rank, leaf_len = basis.shape
    step = 512
    scale = (2.0 * kernel_rate) ** 0.5
    for start in range(0, points, step):
        cols = pl.ds(start, step)
        pts = coords[:, cols] * scale
        hi, mid, lo = split3(pts)
        n_hi, n_mid, n_lo = split3(-0.5 * jnp.sum(pts * pts, axis=0, keepdims=True))
        left = WIDTH - rhs - 6 * dim
        row = lax.broadcasted_iota(jnp.int32, (left, step), 0)
        tail = jnp.where(row < 6, 1.0, 0.0)
        tail = jnp.where(row == 0, n_hi, jnp.where(row == 1, n_mid, jnp.where(row == 2, n_lo, tail)))
        whole = jnp.concatenate([charges[:, cols].astype(f32), hi, hi, mid, hi, lo, mid, tail], axis=0)
        src[cols, :] = whole.T

    @pl.loop(0, points // UNROLL)
    def _(block):
        base = pl.multiple_of(block * UNROLL, UNROLL)
        got = [src[pl.ds(order[base + u], 1), :] for u in range(UNROLL)]
        for u in range(UNROLL):
            dst[pl.ds(base + u, 1), :] = got[u]

    total = jnp.zeros((rhs, rank), f32)
    for j in range(leaves):
        span = pl.ds(j * leaf_len, leaf_len)
        mine = dst[span, :].astype(bf16)
        rows_out[span, :] = mine
        skel = dot(basis[j], mine).T[:rhs]
        skel_out[j] = skel
        total = total + dot_split(skel, transfer[j])
    for k in range(factors.shape[0]):
        terms_out[k] = dot_split(total, factors[k, 0])


def partner(levels_leaf, k):
    axis, bit = ("leaf", k) if k < levels_leaf else ("top", k - levels_leaf)
    me, stride = lax.axis_index(axis), 2**bit
    return {axis: me + stride - 2 * stride * lax.rem(lax.div(me, stride), 2)}


def field_kernel(
    levels_leaf, rows, skel, terms, basis, leaf_factors, transfer, factors, out, right, local, got, held, send, recv
):
    levels, rhs, rank = terms.shape
    leaves, _, leaf_len = basis.shape
    barrier = pltpu.get_barrier_semaphore()
    for k in range(levels):
        pl.semaphore_signal(barrier, inc=1, device_id=partner(levels_leaf, k), device_id_type=MESH)
    pl.semaphore_wait(barrier, levels)

    copies = {}

    def start(k, level):
        copies[k, level] = pltpu.make_async_remote_copy(
            src_ref=terms.at[level] if k == 0 else held.at[k, level],
            dst_ref=got.at[k, level],
            send_sem=send.at[k, level],
            recv_sem=recv.at[k, level],
            device_id=partner(levels_leaf, k),
            device_id_type=MESH,
        )
        copies[k, level].start()

    for level in reversed(range(levels)):
        start(0, level)

    coeffs = [jnp.zeros((rhs, rank), f32)]

    def receive(k, level):
        copies[k, level].wait_recv()
        if level == k:
            coeffs[0] = coeffs[0] + dot_split(got[k, k] * 0.5 ** (k / 2.0), factors[k, 1])
        else:
            held[k + 1, level] = (terms[level] if k == 0 else held[k, level]) + got[k, level]
            start(k + 1, level)

    def right_rows(j):
        lane = lax.broadcasted_iota(jnp.int32, (WIDTH, WIDTH), 1)
        lane_in = lax.broadcasted_iota(jnp.int32, (WIDTH, WIDTH), 0)
        dim = 8
        tail = rhs + 6 * dim
        source = lane
        for slot, shift in ((1, dim), (2, -2 * dim), (3, dim), (4, -4 * dim)):
            low = rhs + slot * dim
            source = jnp.where((lane >= low) & (lane < low + dim), lane + shift, source)
        source = jnp.where((lane >= tail) & (lane < tail + 3), lane + 3, source)
        source = jnp.where((lane >= tail + 3) & (lane < tail + 6), lane - 3, source)
        source = jnp.where((lane < rhs) | (lane >= tail + 6), -1, source)
        chosen = jnp.where(lane_in == source, 1.0, 0.0).astype(bf16)
        span = pl.ds(j * leaf_len, leaf_len)
        right[span, :] = dot(rows[span, :], chosen).astype(bf16)

    def near(j, start_row):
        span = pl.ds(j * leaf_len, leaf_len)
        mine = pl.ds(j * leaf_len + start_row, ROWS)
        power = dot(rows[mine, :], right[span, :], ((1,), (1,)))
        out[mine, :] = dot(jnp.exp(power).astype(bf16), rows[span, :])

    def local_terms(h):
        width = 2**h
        part = [dot_split(skel[j], leaf_factors[j, h, 0]) for j in range(leaves)]
        for j in range(leaves):
            other = (j // width ^ 1) * width
            summed = part[other]
            for i in range(1, width):
                summed = summed + part[other + i]
            mine = dot_split(summed * 0.5 ** (h / 2.0), leaf_factors[j, h, 1])
            local[j] = mine if h == 0 else local[j] + mine

    tasks = [functools.partial(right_rows, j) for j in range(leaves)]
    tasks += [functools.partial(local_terms, h) for h in range(leaf_factors.shape[1])]
    tasks += [functools.partial(near, j, s) for j in range(leaves) for s in range(0, leaf_len, ROWS)]
    events = [(k, level) for k in range(levels) for level in reversed(range(k, levels))]
    done = 0
    for i, task in enumerate(tasks):
        task()
        while done < len(events) * (i + 1) // len(tasks):
            receive(*events[done])
            done += 1
    for copy in copies.values():
        copy.wait_send()

    hi = coeffs[0].astype(bf16)
    lo = (coeffs[0] - hi.astype(f32)).astype(bf16)
    for j in range(leaves):
        span = pl.ds(j * leaf_len, leaf_len)
        mine = dot(transfer[j], hi, ((1,), (1,))) + dot(transfer[j], lo, ((1,), (1,)))
        mine = (mine + local[j].T).astype(bf16)
        out[span, :rhs] = out[span, :rhs] + dot(basis[j], mine, ((0,), (0,)))


def place_kernel(order, field, out, dst):
    rhs, points = out.shape

    @pl.loop(0, points // UNROLL)
    def _(block):
        base = pl.multiple_of(block * UNROLL, UNROLL)
        got = [field[pl.ds(base + u, 1), :] for u in range(UNROLL)]
        for u in range(UNROLL):
            dst[pl.ds(order[base + u], 1), :] = got[u]

    step = 512
    for start in range(0, points, step):
        out[:, pl.ds(start, step)] = dst[pl.ds(start, step), :].T[:rhs].astype(bf16)


def params(**more):
    return pltpu.CompilerParams(vmem_limit_bytes=28 * 2**20, **more)


def per_device(coords, order, charges, leaf_basis, leaf_factors, transfer, block_factors):
    coords, order, charges, basis = coords[0, 0], order[0, 0], charges[0, 0], leaf_basis[0, 0]
    leaf_factors, transfer, factors = leaf_factors[0, 0], transfer[0, 0], block_factors[0, 0]
    rhs, points = charges.shape
    leaves, rank, leaf_len = basis.shape
    levels = factors.shape[0]
    rows, skel, terms = pl.pallas_call(
        up_kernel,
        out_shape=(
            jax.ShapeDtypeStruct((points, WIDTH), bf16),
            jax.ShapeDtypeStruct((leaves, rhs, rank), f32),
            jax.ShapeDtypeStruct((levels, rhs, rank), f32),
        ),
        in_specs=[SMEM] + [VMEM] * 5,
        out_specs=(VMEM, VMEM, VMEM),
        scratch_shapes=[pltpu.VMEM((points, WIDTH), f32), pltpu.VMEM((points, WIDTH), f32)],
        compiler_params=params(),
        name="up",
    )(order, coords, charges, basis, transfer, factors)
    levels_leaf = lax.axis_size("leaf").bit_length() - 1
    field = pl.pallas_call(
        functools.partial(field_kernel, levels_leaf),
        out_shape=jax.ShapeDtypeStruct((points, WIDTH), f32),
        in_specs=[VMEM] * 7,
        out_specs=VMEM,
        scratch_shapes=[
            pltpu.VMEM((points, WIDTH), bf16),
            pltpu.VMEM((leaves, rhs, rank), f32),
            pltpu.VMEM((levels, levels, rhs, rank), f32),
            pltpu.VMEM((levels, levels, rhs, rank), f32),
            pltpu.SemaphoreType.DMA((levels, levels)),
            pltpu.SemaphoreType.DMA((levels, levels)),
        ],
        compiler_params=params(collective_id=0, has_side_effects=True),
        name="field",
    )(rows, skel, terms, basis, leaf_factors, transfer, factors)
    result = pl.pallas_call(
        place_kernel,
        out_shape=jax.ShapeDtypeStruct((rhs, points), bf16),
        in_specs=[SMEM, VMEM],
        out_specs=VMEM,
        scratch_shapes=[pltpu.VMEM((points, WIDTH), f32)],
        compiler_params=params(),
        name="place",
    )(order, field)
    return result[None, None]


def solution(mesh):
    return jax.shard_map(
        per_device,
        mesh=mesh,
        in_specs=(
            P("top", "leaf", None, None),
            P("top", "leaf", None),
            P("top", "leaf", None, None),
            P("top", "leaf", None, None, None),
            P("top", "leaf", None, None, None, None, None),
            P("top", "leaf", None, None, None),
            P("top", "leaf", None, None, None, None),
        ),
        out_specs=P("top", "leaf", None, None),
        check_vma=False,
    )
```

```python
import functools

import jax
import jax.numpy as jnp
from jax import lax
from jax.experimental import pallas as pl
from jax.experimental.pallas import tpu as pltpu
from jax.sharding import PartitionSpec as P

kernel_rate = 4.0
WIDTH = 128
UNROLL = 32
ROWS = 256
MESH = pl.DeviceIdType.MESH
VMEM = pl.BlockSpec(memory_space=pltpu.VMEM)
SMEM = pl.BlockSpec(memory_space=pltpu.SMEM)
f32, bf16 = jnp.float32, jnp.bfloat16


def split3(x):
    hi = x.astype(bf16).astype(f32)
    mid = (x - hi).astype(bf16).astype(f32)
    lo = (x - hi - mid).astype(bf16).astype(f32)
    return hi, mid, lo


def dot(a, b, dims=((1,), (0,))):
    return lax.dot_general(a, b, (dims, ((), ())), preferred_element_type=f32)


def dot_split(x, w):
    hi = x.astype(bf16)
    lo = (x - hi.astype(f32)).astype(bf16)
    return dot(hi, w) + dot(lo, w)


def up_kernel(*refs):
    given, (rows_out, skel_out, terms_out), (src, dst) = refs[:6], refs[6:9], refs[9:11]
    held, sems = refs[11:17], refs[17]
    order, coords, charges, basis, transfer, factors = held
    copies = [pltpu.make_async_copy(a, b, sems.at[i]) for i, (a, b) in enumerate(zip(given, held))]
    for i in (1, 2, 0, 3, 4, 5):
        copies[i].start()
    copies[1].wait()
    copies[2].wait()
    rhs, points = charges.shape
    dim = coords.shape[0]
    leaves, rank, leaf_len = basis.shape
    step = 512
    scale = (2.0 * kernel_rate) ** 0.5
    for start in range(0, points, step):
        cols = pl.ds(start, step)
        pts = coords[:, cols] * scale
        hi, mid, lo = split3(pts)
        n_hi, n_mid, n_lo = split3(-0.5 * jnp.sum(pts * pts, axis=0, keepdims=True))
        left = WIDTH - rhs - 6 * dim
        row = lax.broadcasted_iota(jnp.int32, (left, step), 0)
        tail = jnp.where(row < 6, 1.0, 0.0)
        tail = jnp.where(row == 0, n_hi, jnp.where(row == 1, n_mid, jnp.where(row == 2, n_lo, tail)))
        whole = jnp.concatenate([charges[:, cols].astype(f32), hi, hi, mid, hi, lo, mid, tail], axis=0)
        src[cols, :] = whole.T

    copies[0].wait()

    @pl.loop(0, points // UNROLL)
    def _(block):
        base = pl.multiple_of(block * UNROLL, UNROLL)
        got = [src[pl.ds(order[base + u], 1), :] for u in range(UNROLL)]
        for u in range(UNROLL):
            dst[pl.ds(base + u, 1), :] = got[u]

    for i in (3, 4, 5):
        copies[i].wait()
    total = jnp.zeros((rhs, rank), f32)
    for j in range(leaves):
        span = pl.ds(j * leaf_len, leaf_len)
        mine = dst[span, :].astype(bf16)
        rows_out[span, :] = mine
        skel = dot(basis[j], mine).T[:rhs]
        skel_out[j] = skel
        total = total + dot_split(skel, transfer[j])
    for k in range(factors.shape[0]):
        terms_out[k] = dot_split(total, factors[k, 0])


def partner(levels_leaf, k):
    axis, bit = ("leaf", k) if k < levels_leaf else ("top", k - levels_leaf)
    me, stride = lax.axis_index(axis), 2**bit
    return {axis: me + stride - 2 * stride * lax.rem(lax.div(me, stride), 2)}


def field_kernel(
    levels_leaf, rows, skel, terms, basis, leaf_factors, transfer, factors, out, right, local, got, held, send, recv
):
    levels, rhs, rank = terms.shape
    leaves, _, leaf_len = basis.shape
    barrier = pltpu.get_barrier_semaphore()
    for k in range(levels):
        pl.semaphore_signal(barrier, inc=1, device_id=partner(levels_leaf, k), device_id_type=MESH)
    pl.semaphore_wait(barrier, levels)

    copies = {}

    def start(k, level):
        copies[k, level] = pltpu.make_async_remote_copy(
            src_ref=terms.at[level] if k == 0 else held.at[k, level],
            dst_ref=got.at[k, level],
            send_sem=send.at[k, level],
            recv_sem=recv.at[k, level],
            device_id=partner(levels_leaf, k),
            device_id_type=MESH,
        )
        copies[k, level].start()

    for level in reversed(range(levels)):
        start(0, level)

    coeffs = [jnp.zeros((rhs, rank), f32)]

    def receive(k, level):
        copies[k, level].wait_recv()
        if level == k:
            coeffs[0] = coeffs[0] + dot_split(got[k, k] * 0.5 ** (k / 2.0), factors[k, 1])
        else:
            held[k + 1, level] = (terms[level] if k == 0 else held[k, level]) + got[k, level]
            start(k + 1, level)

    def right_rows(j):
        lane = lax.broadcasted_iota(jnp.int32, (WIDTH, WIDTH), 1)
        lane_in = lax.broadcasted_iota(jnp.int32, (WIDTH, WIDTH), 0)
        dim = 8
        tail = rhs + 6 * dim
        source = lane
        for slot, shift in ((1, dim), (2, -2 * dim), (3, dim), (4, -4 * dim)):
            low = rhs + slot * dim
            source = jnp.where((lane >= low) & (lane < low + dim), lane + shift, source)
        source = jnp.where((lane >= tail) & (lane < tail + 3), lane + 3, source)
        source = jnp.where((lane >= tail + 3) & (lane < tail + 6), lane - 3, source)
        source = jnp.where((lane < rhs) | (lane >= tail + 6), -1, source)
        chosen = jnp.where(lane_in == source, 1.0, 0.0).astype(bf16)
        span = pl.ds(j * leaf_len, leaf_len)
        right[span, :] = dot(rows[span, :], chosen).astype(bf16)

    def near(j, start_row):
        span = pl.ds(j * leaf_len, leaf_len)
        mine = pl.ds(j * leaf_len + start_row, ROWS)
        power = dot(rows[mine, :], right[span, :], ((1,), (1,)))
        out[mine, :] = dot(jnp.exp(power).astype(bf16), rows[span, :])

    def local_terms(h):
        width = 2**h
        part = [dot_split(skel[j], leaf_factors[j, h, 0]) for j in range(leaves)]
        for j in range(leaves):
            other = (j // width ^ 1) * width
            summed = part[other]
            for i in range(1, width):
                summed = summed + part[other + i]
            mine = dot_split(summed * 0.5 ** (h / 2.0), leaf_factors[j, h, 1])
            local[j] = mine if h == 0 else local[j] + mine

    tasks = [functools.partial(right_rows, j) for j in range(leaves)]
    tasks += [functools.partial(local_terms, h) for h in range(leaf_factors.shape[1])]
    tasks += [functools.partial(near, j, s) for j in range(leaves) for s in range(0, leaf_len, ROWS)]
    events = [(k, level) for k in range(levels) for level in range(k, levels)]
    events.sort(key=lambda event: (2 * event[0] + levels - 1 - event[1], event[0]))
    first = leaves + leaf_factors.shape[1]
    done = 0
    for i, task in enumerate(tasks):
        task()
        while done < len(events) * (i + 1 - first) // (len(tasks) - first):
            receive(*events[done])
            done += 1
    for copy in copies.values():
        copy.wait_send()

    hi = coeffs[0].astype(bf16)
    lo = (coeffs[0] - hi.astype(f32)).astype(bf16)
    for j in range(leaves):
        span = pl.ds(j * leaf_len, leaf_len)
        mine = dot(transfer[j], hi, ((1,), (1,))) + dot(transfer[j], lo, ((1,), (1,)))
        mine = (mine + local[j].T).astype(bf16)
        out[span, :rhs] = out[span, :rhs] + dot(basis[j], mine, ((0,), (0,)))


def place_kernel(order, field, out, dst):
    rhs, points = out.shape

    @pl.loop(0, points // UNROLL)
    def _(block):
        base = pl.multiple_of(block * UNROLL, UNROLL)
        got = [field[pl.ds(base + u, 1), :] for u in range(UNROLL)]
        for u in range(UNROLL):
            dst[pl.ds(order[base + u], 1), :] = got[u]

    step = 512
    for start in range(0, points, step):
        out[:, pl.ds(start, step)] = dst[pl.ds(start, step), :].T[:rhs].astype(bf16)


def params(**more):
    return pltpu.CompilerParams(vmem_limit_bytes=28 * 2**20, **more)


def per_device(coords, order, charges, leaf_basis, leaf_factors, transfer, block_factors):
    coords, order, charges, basis = coords[0, 0], order[0, 0], charges[0, 0], leaf_basis[0, 0]
    leaf_factors, transfer, factors = leaf_factors[0, 0], transfer[0, 0], block_factors[0, 0]
    rhs, points = charges.shape
    leaves, rank, leaf_len = basis.shape
    levels = factors.shape[0]
    rows, skel, terms = pl.pallas_call(
        up_kernel,
        out_shape=(
            jax.ShapeDtypeStruct((points, WIDTH), bf16),
            jax.ShapeDtypeStruct((leaves, rhs, rank), f32),
            jax.ShapeDtypeStruct((levels, rhs, rank), f32),
        ),
        in_specs=[pl.BlockSpec(memory_space=pltpu.HBM)] * 6,
        out_specs=(VMEM, VMEM, VMEM),
        scratch_shapes=[
            pltpu.VMEM((points, WIDTH), f32),
            pltpu.VMEM((points, WIDTH), f32),
            pltpu.SMEM(order.shape, order.dtype),
            *[pltpu.VMEM(a.shape, a.dtype) for a in (coords, charges, basis, transfer, factors)],
            pltpu.SemaphoreType.DMA((6,)),
        ],
        compiler_params=params(),
        name="up",
    )(order, coords, charges, basis, transfer, factors)
    levels_leaf = lax.axis_size("leaf").bit_length() - 1
    field = pl.pallas_call(
        functools.partial(field_kernel, levels_leaf),
        out_shape=jax.ShapeDtypeStruct((points, WIDTH), f32),
        in_specs=[VMEM] * 7,
        out_specs=VMEM,
        scratch_shapes=[
            pltpu.VMEM((points, WIDTH), bf16),
            pltpu.VMEM((leaves, rhs, rank), f32),
            pltpu.VMEM((levels, levels, rhs, rank), f32),
            pltpu.VMEM((levels, levels, rhs, rank), f32),
            pltpu.SemaphoreType.DMA((levels, levels)),
            pltpu.SemaphoreType.DMA((levels, levels)),
        ],
        compiler_params=params(collective_id=0, has_side_effects=True),
        name="field",
    )(rows, skel, terms, basis, leaf_factors, transfer, factors)
    result = pl.pallas_call(
        place_kernel,
        out_shape=jax.ShapeDtypeStruct((rhs, points), bf16),
        in_specs=[SMEM, VMEM],
        out_specs=VMEM,
        scratch_shapes=[pltpu.VMEM((points, WIDTH), f32)],
        compiler_params=params(),
        name="place",
    )(order, field)
    return result[None, None]


def solution(mesh):
    return jax.shard_map(
        per_device,
        mesh=mesh,
        in_specs=(
            P("top", "leaf", None, None),
            P("top", "leaf", None),
            P("top", "leaf", None, None),
            P("top", "leaf", None, None, None),
            P("top", "leaf", None, None, None, None, None),
            P("top", "leaf", None, None, None),
            P("top", "leaf", None, None, None, None),
        ),
        out_specs=P("top", "leaf", None, None),
        check_vma=False,
    )
```

```python
import functools

import jax
import jax.numpy as jnp
from jax import lax
from jax.experimental import pallas as pl
from jax.experimental.pallas import tpu as pltpu
from jax.sharding import PartitionSpec as P

kernel_rate = 4.0
WIDTH = 128
UNROLL = 32
ROWS = 256
MESH = pl.DeviceIdType.MESH
VMEM = pl.BlockSpec(memory_space=pltpu.VMEM)
SMEM = pl.BlockSpec(memory_space=pltpu.SMEM)
f32, bf16 = jnp.float32, jnp.bfloat16


def split3(x):
    hi = x.astype(bf16).astype(f32)
    mid = (x - hi).astype(bf16).astype(f32)
    lo = (x - hi - mid).astype(bf16).astype(f32)
    return hi, mid, lo


def dot(a, b, dims=((1,), (0,))):
    return lax.dot_general(a, b, (dims, ((), ())), preferred_element_type=f32)


def dot_split(x, w):
    hi = x.astype(bf16)
    lo = (x - hi.astype(f32)).astype(bf16)
    return dot(hi, w) + dot(lo, w)


def gather_kernel(order, coords, charges, rows_out, src, dst):
    rhs, points = charges.shape
    dim = coords.shape[0]
    step = 512
    scale = (2.0 * kernel_rate) ** 0.5
    for start in range(0, points, step):
        cols = pl.ds(start, step)
        pts = coords[:, cols] * scale
        hi, mid, lo = split3(pts)
        n_hi, n_mid, n_lo = split3(-0.5 * jnp.sum(pts * pts, axis=0, keepdims=True))
        left = WIDTH - rhs - 6 * dim
        row = lax.broadcasted_iota(jnp.int32, (left, step), 0)
        tail = jnp.where(row < 6, 1.0, 0.0)
        tail = jnp.where(row == 0, n_hi, jnp.where(row == 1, n_mid, jnp.where(row == 2, n_lo, tail)))
        whole = jnp.concatenate([charges[:, cols].astype(f32), hi, hi, mid, hi, lo, mid, tail], axis=0)
        src[cols, :] = whole.T

    @pl.loop(0, points // UNROLL)
    def _(block):
        base = pl.multiple_of(block * UNROLL, UNROLL)
        got = [src[pl.ds(order[base + u], 1), :] for u in range(UNROLL)]
        for u in range(UNROLL):
            dst[pl.ds(base + u, 1), :] = got[u]

    rows_out[...] = dst[...].astype(bf16)


def partner(levels_leaf, k):
    axis, bit = ("leaf", k) if k < levels_leaf else ("top", k - levels_leaf)
    me, stride = lax.axis_index(axis), 2**bit
    return {axis: me + stride - 2 * stride * lax.rem(lax.div(me, stride), 2)}


def field_kernel(
    levels_leaf,
    rows,
    basis,
    leaf_factors,
    transfer,
    factors,
    out,
    skel,
    terms,
    right,
    basis_t,
    local,
    got,
    held,
    send,
    recv,
):
    levels, rhs, rank = terms.shape
    leaves, _, leaf_len = basis.shape
    barrier = pltpu.get_barrier_semaphore()
    for k in range(levels):
        pl.semaphore_signal(barrier, inc=1, device_id=partner(levels_leaf, k), device_id_type=MESH)
    total = jnp.zeros((rhs, rank), f32)
    for j in range(leaves):
        mine = dot(basis[j], rows[pl.ds(j * leaf_len, leaf_len), :]).T[:rhs]
        skel[j] = mine
        total = total + dot_split(mine, transfer[j])
    for k in range(levels):
        terms[k] = dot_split(total, factors[k, 0])
    pl.semaphore_wait(barrier, levels)

    copies = {}

    def start(k, level):
        copies[k, level] = pltpu.make_async_remote_copy(
            src_ref=terms.at[level] if k == 0 else held.at[k, level],
            dst_ref=got.at[k, level],
            send_sem=send.at[k, level],
            recv_sem=recv.at[k, level],
            device_id=partner(levels_leaf, k),
            device_id_type=MESH,
        )
        copies[k, level].start()

    for level in reversed(range(levels)):
        start(0, level)

    coeffs = [jnp.zeros((rhs, rank), f32)]

    def receive(k, level):
        copies[k, level].wait_recv()
        if level == k:
            coeffs[0] = coeffs[0] + dot_split(got[k, k] * 0.5 ** (k / 2.0), factors[k, 1])
        else:
            held[k + 1, level] = (terms[level] if k == 0 else held[k, level]) + got[k, level]
            start(k + 1, level)

    def right_rows(j):
        lane = lax.broadcasted_iota(jnp.int32, (WIDTH, WIDTH), 0)
        lane_in = lax.broadcasted_iota(jnp.int32, (WIDTH, WIDTH), 1)
        dim = 8
        tail = rhs + 6 * dim
        source = lane
        for slot, shift in ((1, dim), (2, -2 * dim), (3, dim), (4, -4 * dim)):
            low = rhs + slot * dim
            source = jnp.where((lane >= low) & (lane < low + dim), lane + shift, source)
        source = jnp.where((lane >= tail) & (lane < tail + 3), lane + 3, source)
        source = jnp.where((lane >= tail + 3) & (lane < tail + 6), lane - 3, source)
        source = jnp.where((lane < rhs) | (lane >= tail + 6), -1, source)
        chosen = jnp.where(lane_in == source, 1.0, 0.0).astype(bf16)
        right[j] = dot(chosen, rows[pl.ds(j * leaf_len, leaf_len), :], ((1,), (1,))).astype(bf16)

    def turn_basis(j):
        basis_t[j] = basis[j].T

    def near(j, start_row):
        span = pl.ds(j * leaf_len, leaf_len)
        mine = pl.ds(j * leaf_len + start_row, ROWS)
        power = dot(rows[mine, :], right[j])
        out[mine, :] = dot(jnp.exp(power).astype(bf16), rows[span, :])

    def local_terms(h):
        width = 2**h
        part = [dot_split(skel[j], leaf_factors[j, h, 0]) for j in range(leaves)]
        for j in range(leaves):
            other = (j // width ^ 1) * width
            summed = part[other]
            for i in range(1, width):
                summed = summed + part[other + i]
            mine = dot_split(summed * 0.5 ** (h / 2.0), leaf_factors[j, h, 1])
            local[j] = mine if h == 0 else local[j] + mine

    tasks = [functools.partial(right_rows, j) for j in range(leaves)]
    tasks += [functools.partial(turn_basis, j) for j in range(leaves)]
    tasks += [functools.partial(local_terms, h) for h in range(leaf_factors.shape[1])]
    tasks += [functools.partial(near, j, s) for j in range(leaves) for s in range(0, leaf_len, ROWS)]
    events = [(k, level) for k in range(levels) for level in range(k, levels)]
    events.sort(key=lambda event: (2 * event[0] + levels - 1 - event[1], event[0]))
    first = 2 * leaves + leaf_factors.shape[1]
    done = 0
    for i, task in enumerate(tasks):
        task()
        while done < len(events) * (i + 1 - first) // (len(tasks) - first):
            receive(*events[done])
            done += 1
    for copy in copies.values():
        copy.wait_send()

    whole = coeffs[0].T
    hi = whole.astype(bf16)
    lo = (whole - hi.astype(f32)).astype(bf16)
    for j in range(leaves):
        span = pl.ds(j * leaf_len, leaf_len)
        mine = (dot(transfer[j], hi) + dot(transfer[j], lo) + local[j].T).astype(bf16)
        out[span, :rhs] = out[span, :rhs] + dot(basis_t[j], mine)


def place_kernel(order, field, out, dst):
    rhs, points = out.shape

    @pl.loop(0, points // UNROLL)
    def _(block):
        base = pl.multiple_of(block * UNROLL, UNROLL)
        got = [field[pl.ds(base + u, 1), :] for u in range(UNROLL)]
        for u in range(UNROLL):
            dst[pl.ds(order[base + u], 1), :] = got[u]

    step = 512
    for start in range(0, points, step):
        out[:, pl.ds(start, step)] = dst[pl.ds(start, step), :].T[:rhs].astype(bf16)


def params(**more):
    return pltpu.CompilerParams(vmem_limit_bytes=28 * 2**20, **more)


def per_device(coords, order, charges, leaf_basis, leaf_factors, transfer, block_factors):
    coords, order, charges, basis = coords[0, 0], order[0, 0], charges[0, 0], leaf_basis[0, 0]
    leaf_factors, transfer, factors = leaf_factors[0, 0], transfer[0, 0], block_factors[0, 0]
    rhs, points = charges.shape
    leaves, rank, leaf_len = basis.shape
    levels = factors.shape[0]
    rows = pl.pallas_call(
        gather_kernel,
        out_shape=jax.ShapeDtypeStruct((points, WIDTH), bf16),
        in_specs=[SMEM, VMEM, VMEM],
        out_specs=VMEM,
        scratch_shapes=[pltpu.VMEM((points, WIDTH), f32), pltpu.VMEM((points, WIDTH), f32)],
        compiler_params=params(),
        name="gather",
    )(order, coords, charges)
    levels_leaf = lax.axis_size("leaf").bit_length() - 1
    field = pl.pallas_call(
        functools.partial(field_kernel, levels_leaf),
        out_shape=jax.ShapeDtypeStruct((points, WIDTH), f32),
        in_specs=[VMEM] * 5,
        out_specs=VMEM,
        scratch_shapes=[
            pltpu.VMEM((leaves, rhs, rank), f32),
            pltpu.VMEM((levels, rhs, rank), f32),
            pltpu.VMEM((leaves, WIDTH, leaf_len), bf16),
            pltpu.VMEM((leaves, leaf_len, rank), bf16),
            pltpu.VMEM((leaves, rhs, rank), f32),
            pltpu.VMEM((levels, levels, rhs, rank), f32),
            pltpu.VMEM((levels, levels, rhs, rank), f32),
            pltpu.SemaphoreType.DMA((levels, levels)),
            pltpu.SemaphoreType.DMA((levels, levels)),
        ],
        compiler_params=params(collective_id=0, has_side_effects=True),
        name="field",
    )(rows, basis, leaf_factors, transfer, factors)
    result = pl.pallas_call(
        place_kernel,
        out_shape=jax.ShapeDtypeStruct((rhs, points), bf16),
        in_specs=[SMEM, VMEM],
        out_specs=VMEM,
        scratch_shapes=[pltpu.VMEM((points, WIDTH), f32)],
        compiler_params=params(),
        name="place",
    )(order, field)
    return result[None, None]


def solution(mesh):
    return jax.shard_map(
        per_device,
        mesh=mesh,
        in_specs=(
            P("top", "leaf", None, None),
            P("top", "leaf", None),
            P("top", "leaf", None, None),
            P("top", "leaf", None, None, None),
            P("top", "leaf", None, None, None, None, None),
            P("top", "leaf", None, None, None),
            P("top", "leaf", None, None, None, None),
        ),
        out_specs=P("top", "leaf", None, None),
        check_vma=False,
    )
```

```python
import functools

import jax
import jax.numpy as jnp
from jax import lax
from jax.experimental import pallas as pl
from jax.experimental.pallas import tpu as pltpu
from jax.sharding import PartitionSpec as P

kernel_rate = 4.0
WIDTH = 128
UNROLL = 32
ROWS = 512
MESH = pl.DeviceIdType.MESH
VMEM = pl.BlockSpec(memory_space=pltpu.VMEM)
HBM = pl.BlockSpec(memory_space=pltpu.HBM)
f32, bf16 = jnp.float32, jnp.bfloat16


def split3(x):
    hi = x.astype(bf16).astype(f32)
    mid = (x - hi).astype(bf16).astype(f32)
    lo = (x - hi - mid).astype(bf16).astype(f32)
    return hi, mid, lo


def dot(a, b, dims=((1,), (0,))):
    return lax.dot_general(a, b, (dims, ((), ())), preferred_element_type=f32)


def dot_split(x, w):
    hi = x.astype(bf16)
    lo = (x - hi.astype(f32)).astype(bf16)
    return dot(hi, w) + dot(lo, w)


def partner(levels_leaf, k):
    axis, bit = ("leaf", k) if k < levels_leaf else ("top", k - levels_leaf)
    me, stride = lax.axis_index(axis), 2**bit
    return {axis: me + stride - 2 * stride * lax.rem(lax.div(me, stride), 2)}


def gather_rows(order, coords, charges, rows, src, dst):
    rhs, points = charges.shape
    dim = coords.shape[0]
    step = 512
    scale = (2.0 * kernel_rate) ** 0.5
    for start in range(0, points, step):
        cols = pl.ds(start, step)
        pts = coords[:, cols] * scale
        hi, mid, lo = split3(pts)
        n_hi, n_mid, n_lo = split3(-0.5 * jnp.sum(pts * pts, axis=0, keepdims=True))
        left = WIDTH - rhs - 6 * dim
        row = lax.broadcasted_iota(jnp.int32, (left, step), 0)
        tail = jnp.where(row < 6, 1.0, 0.0)
        tail = jnp.where(row == 0, n_hi, jnp.where(row == 1, n_mid, jnp.where(row == 2, n_lo, tail)))
        whole = jnp.concatenate([charges[:, cols].astype(f32), hi, hi, mid, hi, lo, mid, tail], axis=0)
        src[cols, :] = whole.T

    @pl.loop(0, points // UNROLL)
    def _(block):
        base = pl.multiple_of(block * UNROLL, UNROLL)
        got = [src[pl.ds(order[base + u], 1), :] for u in range(UNROLL)]
        for u in range(UNROLL):
            dst[pl.ds(base + u, 1), :] = got[u]

    rows[...] = dst[...].astype(bf16)


def field_kernel(levels_leaf, *refs):
    given, field, held_in, in_sems = refs[:7], refs[7], refs[8:15], refs[15]
    order, coords, charges, basis, leaf_factors, transfer, factors = held_in
    src, dst, rows, skel, terms, right, basis_t, local, power, out, stage, got, held, send, recv, out_sems = refs[16:]
    levels, rhs, rank = terms.shape
    leaves, _, leaf_len = basis.shape
    inputs = [pltpu.make_async_copy(a, b, in_sems.at[i]) for i, (a, b) in enumerate(zip(given, held_in))]
    for i in (1, 2, 0, 3, 5, 6, 4):
        inputs[i].start()
    barrier = pltpu.get_barrier_semaphore()
    for k in range(levels):
        pl.semaphore_signal(barrier, inc=1, device_id=partner(levels_leaf, k), device_id_type=MESH)
    for i in (1, 2, 0):
        inputs[i].wait()
    gather_rows(order, coords, charges, rows, src, dst)
    for i in (3, 5, 6):
        inputs[i].wait()
    total = jnp.zeros((rhs, rank), f32)
    for j in range(leaves):
        mine = dot(basis[j], rows[pl.ds(j * leaf_len, leaf_len), :]).T[:rhs]
        skel[j] = mine
        total = total + dot_split(mine, transfer[j])
    for k in range(levels):
        terms[k] = dot_split(total, factors[k, 0])
    pl.semaphore_wait(barrier, levels)

    copies = {}

    def start(k, level):
        copies[k, level] = pltpu.make_async_remote_copy(
            src_ref=terms.at[level] if k == 0 else held.at[k, level],
            dst_ref=got.at[k, level],
            send_sem=send.at[k, level],
            recv_sem=recv.at[k, level],
            device_id=partner(levels_leaf, k),
            device_id_type=MESH,
        )
        copies[k, level].start()

    for level in reversed(range(levels)):
        start(0, level)

    coeffs = [jnp.zeros((rhs, rank), f32)]

    def receive(k, level):
        copies[k, level].wait_recv()
        if level == k:
            coeffs[0] = coeffs[0] + dot_split(got[k, k] * 0.5 ** (k / 2.0), factors[k, 1])
        else:
            held[k + 1, level] = (terms[level] if k == 0 else held[k, level]) + got[k, level]
            start(k + 1, level)

    def right_rows(j):
        lane = lax.broadcasted_iota(jnp.int32, (WIDTH, WIDTH), 0)
        lane_in = lax.broadcasted_iota(jnp.int32, (WIDTH, WIDTH), 1)
        dim = 8
        tail = rhs + 6 * dim
        source = lane
        for slot, shift in ((1, dim), (2, -2 * dim), (3, dim), (4, -4 * dim)):
            low = rhs + slot * dim
            source = jnp.where((lane >= low) & (lane < low + dim), lane + shift, source)
        source = jnp.where((lane >= tail) & (lane < tail + 3), lane + 3, source)
        source = jnp.where((lane >= tail + 3) & (lane < tail + 6), lane - 3, source)
        source = jnp.where((lane < rhs) | (lane >= tail + 6), -1, source)
        chosen = jnp.where(lane_in == source, 1.0, 0.0).astype(bf16)
        right[j] = dot(chosen, rows[pl.ds(j * leaf_len, leaf_len), :], ((1,), (1,))).astype(bf16)

    def turn_basis(j):
        basis_t[j] = basis[j].T

    blocks = [(j, start_row) for j in range(leaves) for start_row in range(0, leaf_len, ROWS)]

    def exponent(i):
        j, start_row = blocks[i]
        power[i % 2] = dot(rows[pl.ds(j * leaf_len + start_row, ROWS), :], right[j])

    def near(i):
        j, start_row = blocks[i]
        if i + 1 < len(blocks):
            exponent(i + 1)
        values = jnp.exp(power[i % 2]).astype(bf16)
        out[pl.ds(j * leaf_len + start_row, ROWS), :] = dot(values, rows[pl.ds(j * leaf_len, leaf_len), :])

    def local_terms(h):
        width = 2**h
        part = [dot_split(skel[j], leaf_factors[j, h, 0]) for j in range(leaves)]
        for j in range(leaves):
            other = (j // width ^ 1) * width
            summed = part[other]
            for i in range(1, width):
                summed = summed + part[other + i]
            mine = dot_split(summed * 0.5 ** (h / 2.0), leaf_factors[j, h, 1])
            local[j] = mine if h == 0 else local[j] + mine

    tasks = [functools.partial(right_rows, j) for j in range(leaves)]
    tasks += [functools.partial(turn_basis, j) for j in range(leaves)]
    tasks += [inputs[4].wait]
    tasks += [functools.partial(local_terms, h) for h in range(leaf_factors.shape[1])]
    tasks += [functools.partial(exponent, 0)]
    first = len(tasks)
    tasks += [functools.partial(near, i) for i in range(len(blocks))]
    events = [(k, level) for k in range(levels) for level in range(k, levels)]
    events.sort(key=lambda event: (2 * event[0] + levels - 1 - event[1], event[0]))
    done = 0
    for i, task in enumerate(tasks):
        task()
        while done < len(events) * (i + 1 - first) // (len(tasks) - first):
            receive(*events[done])
            done += 1
    for copy in copies.values():
        copy.wait_send()

    none = jnp.zeros((WIDTH - rhs, rank), f32)
    whole = jnp.concatenate([coeffs[0], none], axis=0).T
    hi = whole.astype(bf16)
    lo = (whole - hi.astype(f32)).astype(bf16)
    leaving = []
    for j in range(leaves):
        span = pl.ds(j * leaf_len, leaf_len)
        own = jnp.concatenate([local[j], none], axis=0).T
        mine = (dot(transfer[j], hi) + dot(transfer[j], lo) + own).astype(bf16)
        stage[span, :] = (out[span, :] + dot(basis_t[j], mine)).astype(bf16)
        leaving.append(pltpu.make_async_copy(stage.at[span, :], field.at[span, :], out_sems.at[j]))
        leaving[j].start()
    for copy in leaving:
        copy.wait()


def place_kernel(order_in, field_in, out, order, field, src, dst, sems):
    rhs, points = out.shape
    pieces = 4
    size = points // pieces
    copies = [pltpu.make_async_copy(order_in, order, sems.at[pieces])]
    for i in range(pieces):
        span = pl.ds(i * size, size)
        copies.append(pltpu.make_async_copy(field_in.at[span, :], field.at[span, :], sems.at[i]))
    for copy in copies:
        copy.start()
    copies[0].wait()
    for i in range(pieces):
        copies[i + 1].wait()
        span = pl.ds(i * size, size)
        src[span, :] = field[span, :].astype(f32)

        @pl.loop(0, size // UNROLL)
        def _(block):
            base = pl.multiple_of(i * size + block * UNROLL, UNROLL)
            got = [src[pl.ds(base + u, 1), :] for u in range(UNROLL)]
            for u in range(UNROLL):
                dst[pl.ds(order[base + u], 1), :] = got[u]

    step = 512
    for start in range(0, points, step):
        out[:, pl.ds(start, step)] = dst[pl.ds(start, step), :].T[:rhs].astype(bf16)


def params(**more):
    return pltpu.CompilerParams(vmem_limit_bytes=60 * 2**20, **more)


def per_device(coords, order, charges, leaf_basis, leaf_factors, transfer, block_factors):
    coords, order, charges, basis = coords[0, 0], order[0, 0], charges[0, 0], leaf_basis[0, 0]
    leaf_factors, transfer, factors = leaf_factors[0, 0], transfer[0, 0], block_factors[0, 0]
    rhs, points = charges.shape
    leaves, rank, leaf_len = basis.shape
    levels = factors.shape[0]
    levels_leaf = lax.axis_size("leaf").bit_length() - 1
    inputs = (order, coords, charges, basis, leaf_factors, transfer, factors)
    in_vmem = [pltpu.VMEM(a.shape, a.dtype) for a in inputs[1:]]
    field = pl.pallas_call(
        functools.partial(field_kernel, levels_leaf),
        out_shape=jax.ShapeDtypeStruct((points, WIDTH), bf16),
        in_specs=[HBM] * len(inputs),
        out_specs=HBM,
        scratch_shapes=[
            pltpu.SMEM(order.shape, order.dtype),
            *in_vmem,
            pltpu.SemaphoreType.DMA((len(inputs),)),
            pltpu.VMEM((points, WIDTH), f32),
            pltpu.VMEM((points, WIDTH), f32),
            pltpu.VMEM((points, WIDTH), bf16),
            pltpu.VMEM((leaves, rhs, rank), f32),
            pltpu.VMEM((levels, rhs, rank), f32),
            pltpu.VMEM((leaves, WIDTH, leaf_len), bf16),
            pltpu.VMEM((leaves, leaf_len, rank), bf16),
            pltpu.VMEM((leaves, rhs, rank), f32),
            pltpu.VMEM((2, ROWS, leaf_len), f32),
            pltpu.VMEM((points, WIDTH), f32),
            pltpu.VMEM((points, WIDTH), bf16),
            pltpu.VMEM((levels, levels, rhs, rank), f32),
            pltpu.VMEM((levels, levels, rhs, rank), f32),
            pltpu.SemaphoreType.DMA((levels, levels)),
            pltpu.SemaphoreType.DMA((levels, levels)),
            pltpu.SemaphoreType.DMA((leaves,)),
        ],
        compiler_params=params(collective_id=0, has_side_effects=True),
        name="field",
    )(*inputs)
    result = pl.pallas_call(
        place_kernel,
        out_shape=jax.ShapeDtypeStruct((rhs, points), bf16),
        in_specs=[HBM, HBM],
        out_specs=VMEM,
        scratch_shapes=[
            pltpu.SMEM(order.shape, order.dtype),
            pltpu.VMEM((points, WIDTH), bf16),
            pltpu.VMEM((points, WIDTH), f32),
            pltpu.VMEM((points, WIDTH), f32),
            pltpu.SemaphoreType.DMA((5,)),
        ],
        compiler_params=params(),
        name="place",
    )(order, field)
    return result[None, None]


def solution(mesh):
    return jax.shard_map(
        per_device,
        mesh=mesh,
        in_specs=(
            P("top", "leaf", None, None),
            P("top", "leaf", None),
            P("top", "leaf", None, None),
            P("top", "leaf", None, None, None),
            P("top", "leaf", None, None, None, None, None),
            P("top", "leaf", None, None, None),
            P("top", "leaf", None, None, None, None),
        ),
        out_specs=P("top", "leaf", None, None),
        check_vma=False,
    )
```

```python
import functools

import jax
import jax.numpy as jnp
from jax import lax
from jax.experimental import pallas as pl
from jax.experimental.pallas import tpu as pltpu
from jax.sharding import PartitionSpec as P

kernel_rate = 4.0
WIDTH = 128
UNROLL = 32
ROWS = 512
MESH = pl.DeviceIdType.MESH
VMEM = pl.BlockSpec(memory_space=pltpu.VMEM)
HBM = pl.BlockSpec(memory_space=pltpu.HBM)
f32, bf16 = jnp.float32, jnp.bfloat16


def split3(x):
    hi = x.astype(bf16).astype(f32)
    mid = (x - hi).astype(bf16).astype(f32)
    lo = (x - hi - mid).astype(bf16).astype(f32)
    return hi, mid, lo


def dot(a, b, dims=((1,), (0,))):
    return lax.dot_general(a, b, (dims, ((), ())), preferred_element_type=f32)


def dot_split(x, w):
    hi = x.astype(bf16)
    lo = (x - hi.astype(f32)).astype(bf16)
    return dot(hi, w) + dot(lo, w)


def set_bits(levels_leaf, levels):
    leaf, top = lax.axis_index("leaf"), lax.axis_index("top")
    total = jnp.int32(0)
    for k in range(levels):
        total = total + (lax.rem(lax.div(leaf, 2**k), 2) if k < levels_leaf else lax.rem(lax.div(top, 2 ** (k - levels_leaf)), 2))
    return total


def partner(levels_leaf, k):
    axis, bit = ("leaf", k) if k < levels_leaf else ("top", k - levels_leaf)
    me, stride = lax.axis_index(axis), 2**bit
    return {axis: me + stride - 2 * stride * lax.rem(lax.div(me, stride), 2)}


def gather_rows(order, coords, charges, rows, src, dst):
    rhs, points = charges.shape
    dim = coords.shape[0]
    step = 512
    scale = (2.0 * kernel_rate) ** 0.5
    for start in range(0, points, step):
        cols = pl.ds(start, step)
        pts = coords[:, cols] * scale
        hi, mid, lo = split3(pts)
        n_hi, n_mid, n_lo = split3(-0.5 * jnp.sum(pts * pts, axis=0, keepdims=True))
        left = WIDTH - rhs - 6 * dim
        row = lax.broadcasted_iota(jnp.int32, (left, step), 0)
        tail = jnp.where(row < 6, 1.0, 0.0)
        tail = jnp.where(row == 0, n_hi, jnp.where(row == 1, n_mid, jnp.where(row == 2, n_lo, tail)))
        whole = jnp.concatenate([charges[:, cols].astype(f32), hi, hi, mid, hi, lo, mid, tail], axis=0)
        src[cols, :] = whole.T

    @pl.loop(0, points // UNROLL)
    def _(block):
        base = pl.multiple_of(block * UNROLL, UNROLL)
        got = [src[pl.ds(order[base + u], 1), :] for u in range(UNROLL)]
        for u in range(UNROLL):
            dst[pl.ds(base + u, 1), :] = got[u]

    rows[...] = dst[...].astype(bf16)


def field_kernel(levels_leaf, *refs):
    given, field, held_in, in_sems = refs[:7], refs[7], refs[8:15], refs[15]
    order, coords, charges, basis, leaf_factors, transfer, factors = held_in
    src, dst, rows, skel, terms, right, basis_t, local, power, out, stage, got, held, send, recv, out_sems = refs[16:]
    levels, rhs, rank = terms.shape
    leaves, _, leaf_len = basis.shape
    inputs = [pltpu.make_async_copy(a, b, in_sems.at[i]) for i, (a, b) in enumerate(zip(given, held_in))]
    for i in (1, 2, 0, 3, 5, 6, 4):
        inputs[i].start()
    barrier = pltpu.get_barrier_semaphore()
    for k in range(levels):
        pl.semaphore_signal(barrier, inc=1, device_id=partner(levels_leaf, k), device_id_type=MESH)
    for i in (1, 2, 0):
        inputs[i].wait()
    gather_rows(order, coords, charges, rows, src, dst)
    for i in (3, 5, 6):
        inputs[i].wait()
    total = jnp.zeros((rhs, rank), f32)
    for j in range(leaves):
        mine = dot(basis[j], rows[pl.ds(j * leaf_len, leaf_len), :]).T[:rhs]
        skel[j] = mine
        total = total + dot_split(mine, transfer[j])
    for k in range(levels):
        terms[k] = dot_split(total, factors[k, 0])
    pl.semaphore_wait(barrier, levels)

    copies = {}

    def start(k, level):
        copies[k, level] = pltpu.make_async_remote_copy(
            src_ref=terms.at[level] if k == 0 else held.at[k, level],
            dst_ref=got.at[k, level],
            send_sem=send.at[k, level],
            recv_sem=recv.at[k, level],
            device_id=partner(levels_leaf, k),
            device_id_type=MESH,
        )
        copies[k, level].start()

    for level in reversed(range(levels)):
        start(0, level)

    coeffs = [jnp.zeros((rhs, rank), f32)]

    def receive(k, level):
        copies[k, level].wait_recv()
        if level == k:
            coeffs[0] = coeffs[0] + dot_split(got[k, k] * 0.5 ** (k / 2.0), factors[k, 1])
        else:
            held[k + 1, level] = (terms[level] if k == 0 else held[k, level]) + got[k, level]
            start(k + 1, level)

    def right_rows(j):
        lane = lax.broadcasted_iota(jnp.int32, (WIDTH, WIDTH), 0)
        lane_in = lax.broadcasted_iota(jnp.int32, (WIDTH, WIDTH), 1)
        dim = 8
        tail = rhs + 6 * dim
        source = lane
        for slot, shift in ((1, dim), (2, -2 * dim), (3, dim), (4, -4 * dim)):
            low = rhs + slot * dim
            source = jnp.where((lane >= low) & (lane < low + dim), lane + shift, source)
        source = jnp.where((lane >= tail) & (lane < tail + 3), lane + 3, source)
        source = jnp.where((lane >= tail + 3) & (lane < tail + 6), lane - 3, source)
        source = jnp.where((lane < rhs) | (lane >= tail + 6), -1, source)
        chosen = jnp.where(lane_in == source, 1.0, 0.0).astype(bf16)
        right[j] = dot(chosen, rows[pl.ds(j * leaf_len, leaf_len), :], ((1,), (1,))).astype(bf16)

    def turn_basis(j):
        basis_t[j] = basis[j].T

    per_leaf = leaf_len // ROWS
    blocks = leaves * per_leaf

    def exponent(i):
        mine = pl.ds(pl.multiple_of(i * ROWS, ROWS), ROWS)
        power[lax.rem(i, 2)] = dot(rows[mine, :], right[lax.div(i, per_leaf)])

    def near(i, carry):
        exponent(jnp.minimum(i + 1, blocks - 1))
        values = jnp.exp(power[lax.rem(i, 2)]).astype(bf16)
        leaf = pl.ds(pl.multiple_of(lax.div(i, per_leaf) * leaf_len, leaf_len), leaf_len)
        out[pl.ds(pl.multiple_of(i * ROWS, ROWS), ROWS), :] = dot(values, rows[leaf, :])
        return carry

    def local_terms(h):
        width = 2**h
        part = [dot_split(skel[j], leaf_factors[j, h, 0]) for j in range(leaves)]
        for j in range(leaves):
            other = (j // width ^ 1) * width
            summed = part[other]
            for i in range(1, width):
                summed = summed + part[other + i]
            mine = dot_split(summed * 0.5 ** (h / 2.0), leaf_factors[j, h, 1])
            local[j] = mine if h == 0 else local[j] + mine

    def prepare():
        for j in range(leaves):
            right_rows(j)
            turn_basis(j)
        for h in range(leaf_factors.shape[1]):
            local_terms(h)
        exponent(jnp.int32(0))

    inputs[4].wait()
    ahead = lax.div(blocks * (levels - set_bits(levels_leaf, levels)), levels)
    pl.when(ahead > 0)(prepare)
    lax.fori_loop(0, ahead, near, 0)
    events = [(k, level) for k in range(levels) for level in range(k, levels)]
    events.sort(key=lambda event: (2 * event[0] + levels - 1 - event[1], event[0]))
    for event in events:
        receive(*event)
    pl.when(ahead == 0)(prepare)
    lax.fori_loop(ahead, blocks, near, 0)
    for copy in copies.values():
        copy.wait_send()

    none = jnp.zeros((WIDTH - rhs, rank), f32)
    whole = jnp.concatenate([coeffs[0], none], axis=0).T
    hi = whole.astype(bf16)
    lo = (whole - hi.astype(f32)).astype(bf16)
    leaving = []
    for j in range(leaves):
        span = pl.ds(j * leaf_len, leaf_len)
        own = jnp.concatenate([local[j], none], axis=0).T
        mine = (dot(transfer[j], hi) + dot(transfer[j], lo) + own).astype(bf16)
        stage[span, :] = (out[span, :] + dot(basis_t[j], mine)).astype(bf16)
        leaving.append(pltpu.make_async_copy(stage.at[span, :], field.at[span, :], out_sems.at[j]))
        leaving[j].start()
    for copy in leaving:
        copy.wait()


def place_kernel(order_in, field_in, out, order, field, src, dst, sems):
    rhs, points = out.shape
    pieces = 4
    size = points // pieces
    copies = [pltpu.make_async_copy(order_in, order, sems.at[pieces])]
    for i in range(pieces):
        span = pl.ds(i * size, size)
        copies.append(pltpu.make_async_copy(field_in.at[span, :], field.at[span, :], sems.at[i]))
    for copy in copies:
        copy.start()
    copies[0].wait()
    for i in range(pieces):
        copies[i + 1].wait()
        span = pl.ds(i * size, size)
        src[span, :] = field[span, :].astype(f32)

        @pl.loop(0, size // UNROLL)
        def _(block):
            base = pl.multiple_of(i * size + block * UNROLL, UNROLL)
            got = [src[pl.ds(base + u, 1), :] for u in range(UNROLL)]
            for u in range(UNROLL):
                dst[pl.ds(order[base + u], 1), :] = got[u]

    step = 512
    for start in range(0, points, step):
        out[:, pl.ds(start, step)] = dst[pl.ds(start, step), :].T[:rhs].astype(bf16)


def params(**more):
    return pltpu.CompilerParams(vmem_limit_bytes=60 * 2**20, **more)


def per_device(coords, order, charges, leaf_basis, leaf_factors, transfer, block_factors):
    coords, order, charges, basis = coords[0, 0], order[0, 0], charges[0, 0], leaf_basis[0, 0]
    leaf_factors, transfer, factors = leaf_factors[0, 0], transfer[0, 0], block_factors[0, 0]
    rhs, points = charges.shape
    leaves, rank, leaf_len = basis.shape
    levels = factors.shape[0]
    levels_leaf = lax.axis_size("leaf").bit_length() - 1
    inputs = (order, coords, charges, basis, leaf_factors, transfer, factors)
    in_vmem = [pltpu.VMEM(a.shape, a.dtype) for a in inputs[1:]]
    field = pl.pallas_call(
        functools.partial(field_kernel, levels_leaf),
        out_shape=jax.ShapeDtypeStruct((points, WIDTH), bf16),
        in_specs=[HBM] * len(inputs),
        out_specs=HBM,
        scratch_shapes=[
            pltpu.SMEM(order.shape, order.dtype),
            *in_vmem,
            pltpu.SemaphoreType.DMA((len(inputs),)),
            pltpu.VMEM((points, WIDTH), f32),
            pltpu.VMEM((points, WIDTH), f32),
            pltpu.VMEM((points, WIDTH), bf16),
            pltpu.VMEM((leaves, rhs, rank), f32),
            pltpu.VMEM((levels, rhs, rank), f32),
            pltpu.VMEM((leaves, WIDTH, leaf_len), bf16),
            pltpu.VMEM((leaves, leaf_len, rank), bf16),
            pltpu.VMEM((leaves, rhs, rank), f32),
            pltpu.VMEM((2, ROWS, leaf_len), f32),
            pltpu.VMEM((points, WIDTH), f32),
            pltpu.VMEM((points, WIDTH), bf16),
            pltpu.VMEM((levels, levels, rhs, rank), f32),
            pltpu.VMEM((levels, levels, rhs, rank), f32),
            pltpu.SemaphoreType.DMA((levels, levels)),
            pltpu.SemaphoreType.DMA((levels, levels)),
            pltpu.SemaphoreType.DMA((leaves,)),
        ],
        compiler_params=params(collective_id=0, has_side_effects=True),
        name="field",
    )(*inputs)
    result = pl.pallas_call(
        place_kernel,
        out_shape=jax.ShapeDtypeStruct((rhs, points), bf16),
        in_specs=[HBM, HBM],
        out_specs=VMEM,
        scratch_shapes=[
            pltpu.SMEM(order.shape, order.dtype),
            pltpu.VMEM((points, WIDTH), bf16),
            pltpu.VMEM((points, WIDTH), f32),
            pltpu.VMEM((points, WIDTH), f32),
            pltpu.SemaphoreType.DMA((5,)),
        ],
        compiler_params=params(),
        name="place",
    )(order, field)
    return result[None, None]


def solution(mesh):
    return jax.shard_map(
        per_device,
        mesh=mesh,
        in_specs=(
            P("top", "leaf", None, None),
            P("top", "leaf", None),
            P("top", "leaf", None, None),
            P("top", "leaf", None, None, None),
            P("top", "leaf", None, None, None, None, None),
            P("top", "leaf", None, None, None),
            P("top", "leaf", None, None, None, None),
        ),
        out_specs=P("top", "leaf", None, None),
        check_vma=False,
    )
```

```python
import functools

import jax
import jax.numpy as jnp
from jax import lax
from jax.experimental import pallas as pl
from jax.experimental.pallas import tpu as pltpu
from jax.sharding import PartitionSpec as P

kernel_rate = 4.0
WIDTH = 128
UNROLL = 32
ROWS = 512
MESH = pl.DeviceIdType.MESH
VMEM = pl.BlockSpec(memory_space=pltpu.VMEM)
HBM = pl.BlockSpec(memory_space=pltpu.HBM)
f32, bf16 = jnp.float32, jnp.bfloat16


def split3(x):
    hi = x.astype(bf16).astype(f32)
    mid = (x - hi).astype(bf16).astype(f32)
    lo = (x - hi - mid).astype(bf16).astype(f32)
    return hi, mid, lo


def dot(a, b, dims=((1,), (0,))):
    return lax.dot_general(a, b, (dims, ((), ())), preferred_element_type=f32)


def dot_split(x, w):
    hi = x.astype(bf16)
    lo = (x - hi.astype(f32)).astype(bf16)
    return dot(hi, w) + dot(lo, w)


def set_bits(levels_leaf, levels):
    leaf, top = lax.axis_index("leaf"), lax.axis_index("top")
    total = jnp.int32(0)
    for k in range(levels):
        total = total + (lax.rem(lax.div(leaf, 2**k), 2) if k < levels_leaf else lax.rem(lax.div(top, 2 ** (k - levels_leaf)), 2))
    return total


def partner(levels_leaf, k):
    axis, bit = ("leaf", k) if k < levels_leaf else ("top", k - levels_leaf)
    me, stride = lax.axis_index(axis), 2**bit
    return {axis: me + stride - 2 * stride * lax.rem(lax.div(me, stride), 2)}


def gather_rows(order, coords, charges, rows, src, dst):
    rhs, points = charges.shape
    dim = coords.shape[0]
    step = 512
    scale = (2.0 * kernel_rate) ** 0.5
    for start in range(0, points, step):
        cols = pl.ds(start, step)
        pts = coords[:, cols] * scale
        hi, mid, lo = split3(pts)
        n_hi, n_mid, n_lo = split3(-0.5 * jnp.sum(pts * pts, axis=0, keepdims=True))
        left = WIDTH - rhs - 6 * dim
        row = lax.broadcasted_iota(jnp.int32, (left, step), 0)
        tail = jnp.where(row < 6, 1.0, 0.0)
        tail = jnp.where(row == 0, n_hi, jnp.where(row == 1, n_mid, jnp.where(row == 2, n_lo, tail)))
        whole = jnp.concatenate([charges[:, cols].astype(f32), hi, hi, mid, hi, lo, mid, tail], axis=0)
        src[cols, :] = whole.T

    @pl.loop(0, points // UNROLL)
    def _(block):
        base = pl.multiple_of(block * UNROLL, UNROLL)
        got = [src[pl.ds(order[base + u], 1), :] for u in range(UNROLL)]
        for u in range(UNROLL):
            dst[pl.ds(base + u, 1), :] = got[u]

    rows[...] = dst[...].astype(bf16)


def field_kernel(levels_leaf, *refs):
    given, field, held_in, in_sems = refs[:7], refs[7], refs[8:15], refs[15]
    order, coords, charges, basis, leaf_factors, transfer, factors = held_in
    src, dst, rows, skel, terms, right, basis_t, local, power, out, stage, got, held, send, recv, out_sems = refs[16:]
    levels, rhs, rank = terms.shape
    leaves, _, leaf_len = basis.shape
    inputs = [pltpu.make_async_copy(a, b, in_sems.at[i]) for i, (a, b) in enumerate(zip(given, held_in))]
    for i in (1, 2, 0, 3, 5, 6, 4):
        inputs[i].start()
    barrier = pltpu.get_barrier_semaphore()
    for k in range(levels):
        pl.semaphore_signal(barrier, inc=1, device_id=partner(levels_leaf, k), device_id_type=MESH)
    for i in (1, 2, 0):
        inputs[i].wait()
    gather_rows(order, coords, charges, rows, src, dst)
    for i in (3, 5, 6):
        inputs[i].wait()
    total = jnp.zeros((rhs, rank), f32)
    for j in range(leaves):
        mine = dot(basis[j], rows[pl.ds(j * leaf_len, leaf_len), :]).T[:rhs]
        skel[j] = mine
        total = total + dot_split(mine, transfer[j])
    for k in range(levels):
        terms[k] = dot_split(total, factors[k, 0])
    pl.semaphore_wait(barrier, levels)

    copies = {}

    def start(k, level):
        copies[k, level] = pltpu.make_async_remote_copy(
            src_ref=terms.at[level] if k == 0 else held.at[k, level],
            dst_ref=got.at[k, level],
            send_sem=send.at[k, level],
            recv_sem=recv.at[k, level],
            device_id=partner(levels_leaf, k),
            device_id_type=MESH,
        )
        copies[k, level].start()

    for level in reversed(range(levels)):
        start(0, level)

    coeffs = [jnp.zeros((rhs, rank), f32)]

    def receive(k, level):
        copies[k, level].wait_recv()
        if level == k:
            coeffs[0] = coeffs[0] + dot_split(got[k, k] * 0.5 ** (k / 2.0), factors[k, 1])
        else:
            held[k + 1, level] = (terms[level] if k == 0 else held[k, level]) + got[k, level]
            start(k + 1, level)

    def right_rows(j):
        lane = lax.broadcasted_iota(jnp.int32, (WIDTH, WIDTH), 0)
        lane_in = lax.broadcasted_iota(jnp.int32, (WIDTH, WIDTH), 1)
        dim = 8
        tail = rhs + 6 * dim
        source = lane
        for slot, shift in ((1, dim), (2, -2 * dim), (3, dim), (4, -4 * dim)):
            low = rhs + slot * dim
            source = jnp.where((lane >= low) & (lane < low + dim), lane + shift, source)
        source = jnp.where((lane >= tail) & (lane < tail + 3), lane + 3, source)
        source = jnp.where((lane >= tail + 3) & (lane < tail + 6), lane - 3, source)
        source = jnp.where((lane < rhs) | (lane >= tail + 6), -1, source)
        chosen = jnp.where(lane_in == source, 1.0, 0.0).astype(bf16)
        right[j] = dot(chosen, rows[pl.ds(j * leaf_len, leaf_len), :], ((1,), (1,))).astype(bf16)

    def turn_basis(j):
        basis_t[j] = basis[j].T

    def near(j):
        leaf = pl.ds(j * leaf_len, leaf_len)
        parts = [pl.ds(j * leaf_len + start_row, ROWS) for start_row in range(0, leaf_len, ROWS)]
        for i, part in enumerate(parts):
            power[i] = dot(rows[part, :], right[j])
        for i, part in enumerate(parts):
            out[part, :] = dot(jnp.exp(power[i]).astype(bf16), rows[leaf, :])

    def local_terms(h):
        width = 2**h
        part = [dot_split(skel[j], leaf_factors[j, h, 0]) for j in range(leaves)]
        for j in range(leaves):
            other = (j // width ^ 1) * width
            summed = part[other]
            for i in range(1, width):
                summed = summed + part[other + i]
            mine = dot_split(summed * 0.5 ** (h / 2.0), leaf_factors[j, h, 1])
            local[j] = mine if h == 0 else local[j] + mine

    def prepare():
        for j in range(leaves):
            right_rows(j)
            turn_basis(j)
        for h in range(leaf_factors.shape[1]):
            local_terms(h)

    inputs[4].wait()
    ahead = lax.div(leaves * (levels - set_bits(levels_leaf, levels)), levels)
    pl.when(ahead > 0)(prepare)
    for j in range(leaves):
        pl.when(ahead > j)(functools.partial(near, j))
    events = [(k, level) for k in range(levels) for level in range(k, levels)]
    events.sort(key=lambda event: (2 * event[0] + levels - 1 - event[1], event[0]))
    for event in events:
        receive(*event)
    pl.when(ahead == 0)(prepare)
    for j in range(leaves):
        pl.when(ahead <= j)(functools.partial(near, j))
    for copy in copies.values():
        copy.wait_send()

    none = jnp.zeros((WIDTH - rhs, rank), f32)
    whole = jnp.concatenate([coeffs[0], none], axis=0).T
    hi = whole.astype(bf16)
    lo = (whole - hi.astype(f32)).astype(bf16)
    leaving = []
    for j in range(leaves):
        span = pl.ds(j * leaf_len, leaf_len)
        own = jnp.concatenate([local[j], none], axis=0).T
        mine = (dot(transfer[j], hi) + dot(transfer[j], lo) + own).astype(bf16)
        stage[span, :] = (out[span, :] + dot(basis_t[j], mine)).astype(bf16)
        leaving.append(pltpu.make_async_copy(stage.at[span, :], field.at[span, :], out_sems.at[j]))
        leaving[j].start()
    for copy in leaving:
        copy.wait()


def place_kernel(order_in, field_in, out, order, field, src, dst, sems):
    rhs, points = out.shape
    pieces = 4
    size = points // pieces
    copies = [pltpu.make_async_copy(order_in, order, sems.at[pieces])]
    for i in range(pieces):
        span = pl.ds(i * size, size)
        copies.append(pltpu.make_async_copy(field_in.at[span, :], field.at[span, :], sems.at[i]))
    for copy in copies:
        copy.start()
    copies[0].wait()
    for i in range(pieces):
        copies[i + 1].wait()
        span = pl.ds(i * size, size)
        src[span, :] = field[span, :].astype(f32)

        @pl.loop(0, size // UNROLL)
        def _(block):
            base = pl.multiple_of(i * size + block * UNROLL, UNROLL)
            got = [src[pl.ds(base + u, 1), :] for u in range(UNROLL)]
            for u in range(UNROLL):
                dst[pl.ds(order[base + u], 1), :] = got[u]

    step = 512
    for start in range(0, points, step):
        out[:, pl.ds(start, step)] = dst[pl.ds(start, step), :].T[:rhs].astype(bf16)


def params(**more):
    return pltpu.CompilerParams(vmem_limit_bytes=60 * 2**20, **more)


def per_device(coords, order, charges, leaf_basis, leaf_factors, transfer, block_factors):
    coords, order, charges, basis = coords[0, 0], order[0, 0], charges[0, 0], leaf_basis[0, 0]
    leaf_factors, transfer, factors = leaf_factors[0, 0], transfer[0, 0], block_factors[0, 0]
    rhs, points = charges.shape
    leaves, rank, leaf_len = basis.shape
    levels = factors.shape[0]
    levels_leaf = lax.axis_size("leaf").bit_length() - 1
    inputs = (order, coords, charges, basis, leaf_factors, transfer, factors)
    in_vmem = [pltpu.VMEM(a.shape, a.dtype) for a in inputs[1:]]
    field = pl.pallas_call(
        functools.partial(field_kernel, levels_leaf),
        out_shape=jax.ShapeDtypeStruct((points, WIDTH), bf16),
        in_specs=[HBM] * len(inputs),
        out_specs=HBM,
        scratch_shapes=[
            pltpu.SMEM(order.shape, order.dtype),
            *in_vmem,
            pltpu.SemaphoreType.DMA((len(inputs),)),
            pltpu.VMEM((points, WIDTH), f32),
            pltpu.VMEM((points, WIDTH), f32),
            pltpu.VMEM((points, WIDTH), bf16),
            pltpu.VMEM((leaves, rhs, rank), f32),
            pltpu.VMEM((levels, rhs, rank), f32),
            pltpu.VMEM((leaves, WIDTH, leaf_len), bf16),
            pltpu.VMEM((leaves, leaf_len, rank), bf16),
            pltpu.VMEM((leaves, rhs, rank), f32),
            pltpu.VMEM((leaf_len // ROWS, ROWS, leaf_len), f32),
            pltpu.VMEM((points, WIDTH), f32),
            pltpu.VMEM((points, WIDTH), bf16),
            pltpu.VMEM((levels, levels, rhs, rank), f32),
            pltpu.VMEM((levels, levels, rhs, rank), f32),
            pltpu.SemaphoreType.DMA((levels, levels)),
            pltpu.SemaphoreType.DMA((levels, levels)),
            pltpu.SemaphoreType.DMA((leaves,)),
        ],
        compiler_params=params(collective_id=0, has_side_effects=True),
        name="field",
    )(*inputs)
    result = pl.pallas_call(
        place_kernel,
        out_shape=jax.ShapeDtypeStruct((rhs, points), bf16),
        in_specs=[HBM, HBM],
        out_specs=VMEM,
        scratch_shapes=[
            pltpu.SMEM(order.shape, order.dtype),
            pltpu.VMEM((points, WIDTH), bf16),
            pltpu.VMEM((points, WIDTH), f32),
            pltpu.VMEM((points, WIDTH), f32),
            pltpu.SemaphoreType.DMA((5,)),
        ],
        compiler_params=params(),
        name="place",
    )(order, field)
    return result[None, None]


def solution(mesh):
    return jax.shard_map(
        per_device,
        mesh=mesh,
        in_specs=(
            P("top", "leaf", None, None),
            P("top", "leaf", None),
            P("top", "leaf", None, None),
            P("top", "leaf", None, None, None),
            P("top", "leaf", None, None, None, None, None),
            P("top", "leaf", None, None, None),
            P("top", "leaf", None, None, None, None),
        ),
        out_specs=P("top", "leaf", None, None),
        check_vma=False,
    )
```

```python
import functools
import math

import jax
import jax.numpy as jnp
from jax import lax
from jax.experimental import pallas as pl
from jax.experimental.pallas import tpu as pltpu
from jax.sharding import PartitionSpec as P

kernel_rate = 4.0
WIDTH = 128
UNROLL = 32
ROWS = 512
MESH = pl.DeviceIdType.MESH
VMEM = pl.BlockSpec(memory_space=pltpu.VMEM)
HBM = pl.BlockSpec(memory_space=pltpu.HBM)
f32, bf16 = jnp.float32, jnp.bfloat16


def split3(x):
    hi = x.astype(bf16).astype(f32)
    mid = (x - hi).astype(bf16).astype(f32)
    lo = (x - hi - mid).astype(bf16).astype(f32)
    return hi, mid, lo


def dot(a, b, dims=((1,), (0,))):
    return lax.dot_general(a, b, (dims, ((), ())), preferred_element_type=f32)


def dot_split(x, w):
    hi = x.astype(bf16)
    lo = (x - hi.astype(f32)).astype(bf16)
    return dot(hi, w) + dot(lo, w)


def partner(levels_leaf, k):
    axis, bit = ("leaf", k) if k < levels_leaf else ("top", k - levels_leaf)
    me, stride = lax.axis_index(axis), 2**bit
    return {axis: me + stride - 2 * stride * lax.rem(lax.div(me, stride), 2)}


def gather_rows(order, coords, charges, rows, src, dst):
    rhs, points = charges.shape
    dim = coords.shape[0]
    step = 512
    scale = (2.0 * kernel_rate / math.log(2.0)) ** 0.5
    for start in range(0, points, step):
        cols = pl.ds(start, step)
        pts = coords[:, cols] * scale
        hi, mid, lo = split3(pts)
        n_hi, n_mid, n_lo = split3(-0.5 * jnp.sum(pts * pts, axis=0, keepdims=True))
        left = WIDTH - rhs - 6 * dim
        row = lax.broadcasted_iota(jnp.int32, (left, step), 0)
        tail = jnp.where(row < 6, 1.0, 0.0)
        tail = jnp.where(row == 0, n_hi, jnp.where(row == 1, n_mid, jnp.where(row == 2, n_lo, tail)))
        whole = jnp.concatenate([charges[:, cols].astype(f32), hi, hi, mid, hi, lo, mid, tail], axis=0)
        src[cols, :] = whole.T

    @pl.loop(0, points // UNROLL)
    def _(block):
        base = pl.multiple_of(block * UNROLL, UNROLL)
        got = [src[pl.ds(order[base + u], 1), :] for u in range(UNROLL)]
        for u in range(UNROLL):
            dst[pl.ds(base + u, 1), :] = got[u]

    rows[...] = dst[...].astype(bf16)


def field_kernel(levels_leaf, *refs):
    given, field, held_in, in_sems = refs[:7], refs[7], refs[8:15], refs[15]
    order, coords, charges, basis, leaf_factors, transfer, factors = held_in
    src, dst, rows, skel, terms, right, basis_t, local, power, out, stage, got, held, send, recv, out_sems = refs[16:]
    levels, rhs, rank = terms.shape
    leaves, _, leaf_len = basis.shape
    inputs = [pltpu.make_async_copy(a, b, in_sems.at[i]) for i, (a, b) in enumerate(zip(given, held_in))]
    for i in (1, 2, 0, 3, 5, 6, 4):
        inputs[i].start()
    barrier = pltpu.get_barrier_semaphore()
    for k in range(levels):
        pl.semaphore_signal(barrier, inc=1, device_id=partner(levels_leaf, k), device_id_type=MESH)
    for i in (1, 2, 0):
        inputs[i].wait()
    gather_rows(order, coords, charges, rows, src, dst)
    for i in (3, 5, 6):
        inputs[i].wait()
    total = jnp.zeros((rhs, rank), f32)
    for j in range(leaves):
        mine = dot(basis[j], rows[pl.ds(j * leaf_len, leaf_len), :]).T[:rhs]
        skel[j] = mine
        total = total + dot_split(mine, transfer[j])
    for k in range(levels):
        terms[k] = dot_split(total, factors[k, 0])
    pl.semaphore_wait(barrier, levels)

    copies = {}

    def start(k, level):
        copies[k, level] = pltpu.make_async_remote_copy(
            src_ref=terms.at[level] if k == 0 else held.at[k, level],
            dst_ref=got.at[k, level],
            send_sem=send.at[k, level],
            recv_sem=recv.at[k, level],
            device_id=partner(levels_leaf, k),
            device_id_type=MESH,
        )
        copies[k, level].start()

    start(0, levels - 1)

    coeffs = [jnp.zeros((rhs, rank), f32)]

    def receive(k, level):
        copies[k, level].wait_recv()
        if level == k:
            coeffs[0] = coeffs[0] + dot_split(got[k, k] * 0.5 ** (k / 2.0), factors[k, 1])
        else:
            held[k + 1, level] = (terms[level] if k == 0 else held[k, level]) + got[k, level]
            start(k + 1, level)

    def right_rows(j):
        lane = lax.broadcasted_iota(jnp.int32, (WIDTH, WIDTH), 0)
        lane_in = lax.broadcasted_iota(jnp.int32, (WIDTH, WIDTH), 1)
        dim = 8
        tail = rhs + 6 * dim
        source = lane
        for slot, shift in ((1, dim), (2, -2 * dim), (3, dim), (4, -4 * dim)):
            low = rhs + slot * dim
            source = jnp.where((lane >= low) & (lane < low + dim), lane + shift, source)
        source = jnp.where((lane >= tail) & (lane < tail + 3), lane + 3, source)
        source = jnp.where((lane >= tail + 3) & (lane < tail + 6), lane - 3, source)
        source = jnp.where((lane < rhs) | (lane >= tail + 6), -1, source)
        chosen = jnp.where(lane_in == source, 1.0, 0.0).astype(bf16)
        right[j] = dot(chosen, rows[pl.ds(j * leaf_len, leaf_len), :], ((1,), (1,))).astype(bf16)

    def turn_basis(j):
        basis_t[j] = basis[j].T

    blocks = [(j, start_row) for j in range(leaves) for start_row in range(0, leaf_len, ROWS)]

    def exponent(i):
        j, start_row = blocks[i]
        power[i % 2] = dot(rows[pl.ds(j * leaf_len + start_row, ROWS), :], right[j])

    def near(i):
        j, start_row = blocks[i]
        if i + 1 < len(blocks):
            exponent(i + 1)
        values = jnp.exp2(power[i % 2]).astype(bf16)
        out[pl.ds(j * leaf_len + start_row, ROWS), :] = dot(values, rows[pl.ds(j * leaf_len, leaf_len), :])

    def local_terms(h):
        width = 2**h
        part = [dot_split(skel[j], leaf_factors[j, h, 0]) for j in range(leaves)]
        for j in range(leaves):
            other = (j // width ^ 1) * width
            summed = part[other]
            for i in range(1, width):
                summed = summed + part[other + i]
            mine = dot_split(summed * 0.5 ** (h / 2.0), leaf_factors[j, h, 1])
            local[j] = mine if h == 0 else local[j] + mine

    for j in range(leaves):
        right_rows(j)
        turn_basis(j)
    exponent(0)
    inputs[4].wait()
    tasks = [functools.partial(local_terms, h) for h in range(leaf_factors.shape[1])]
    tasks += [functools.partial(near, i) for i in range(len(blocks))]
    done = 0
    for turn in range(levels):
        receive(turn, levels - 1)
        if turn < levels - 1:
            start(0, levels - 2 - turn)
        for back in range(1, turn + 1):
            if turn - back <= levels - 1 - back:
                receive(turn - back, levels - 1 - back)
        while done < len(tasks) and done * (levels - 1) < len(tasks) * (turn + 1):
            tasks[done]()
            done += 1
    for copy in copies.values():
        copy.wait_send()

    none = jnp.zeros((WIDTH - rhs, rank), f32)
    whole = jnp.concatenate([coeffs[0], none], axis=0).T
    hi = whole.astype(bf16)
    lo = (whole - hi.astype(f32)).astype(bf16)
    leaving = []
    for j in range(leaves):
        span = pl.ds(j * leaf_len, leaf_len)
        own = jnp.concatenate([local[j], none], axis=0).T
        mine = (dot(transfer[j], hi) + dot(transfer[j], lo) + own).astype(bf16)
        stage[span, :] = (out[span, :] + dot(basis_t[j], mine)).astype(bf16)
        leaving.append(pltpu.make_async_copy(stage.at[span, :], field.at[span, :], out_sems.at[j]))
        leaving[j].start()
    for copy in leaving:
        copy.wait()


def place_kernel(order_in, field_in, out, order, field, src, dst, sems):
    rhs, points = out.shape
    pieces = 4
    size = points // pieces
    copies = [pltpu.make_async_copy(order_in, order, sems.at[pieces])]
    for i in range(pieces):
        span = pl.ds(i * size, size)
        copies.append(pltpu.make_async_copy(field_in.at[span, :], field.at[span, :], sems.at[i]))
    for copy in copies:
        copy.start()
    copies[0].wait()
    for i in range(pieces):
        copies[i + 1].wait()
        span = pl.ds(i * size, size)
        src[span, :] = field[span, :].astype(f32)

        @pl.loop(0, size // UNROLL)
        def _(block):
            base = pl.multiple_of(i * size + block * UNROLL, UNROLL)
            got = [src[pl.ds(base + u, 1), :] for u in range(UNROLL)]
            for u in range(UNROLL):
                dst[pl.ds(order[base + u], 1), :] = got[u]

    step = 512
    for start in range(0, points, step):
        out[:, pl.ds(start, step)] = dst[pl.ds(start, step), :].T[:rhs].astype(bf16)


def params(**more):
    return pltpu.CompilerParams(vmem_limit_bytes=60 * 2**20, **more)


def per_device(coords, order, charges, leaf_basis, leaf_factors, transfer, block_factors):
    coords, order, charges, basis = coords[0, 0], order[0, 0], charges[0, 0], leaf_basis[0, 0]
    leaf_factors, transfer, factors = leaf_factors[0, 0], transfer[0, 0], block_factors[0, 0]
    rhs, points = charges.shape
    leaves, rank, leaf_len = basis.shape
    levels = factors.shape[0]
    levels_leaf = lax.axis_size("leaf").bit_length() - 1
    inputs = (order, coords, charges, basis, leaf_factors, transfer, factors)
    in_vmem = [pltpu.VMEM(a.shape, a.dtype) for a in inputs[1:]]
    field = pl.pallas_call(
        functools.partial(field_kernel, levels_leaf),
        out_shape=jax.ShapeDtypeStruct((points, WIDTH), bf16),
        in_specs=[HBM] * len(inputs),
        out_specs=HBM,
        scratch_shapes=[
            pltpu.SMEM(order.shape, order.dtype),
            *in_vmem,
            pltpu.SemaphoreType.DMA((len(inputs),)),
            pltpu.VMEM((points, WIDTH), f32),
            pltpu.VMEM((points, WIDTH), f32),
            pltpu.VMEM((points, WIDTH), bf16),
            pltpu.VMEM((leaves, rhs, rank), f32),
            pltpu.VMEM((levels, rhs, rank), f32),
            pltpu.VMEM((leaves, WIDTH, leaf_len), bf16),
            pltpu.VMEM((leaves, leaf_len, rank), bf16),
            pltpu.VMEM((leaves, rhs, rank), f32),
            pltpu.VMEM((2, ROWS, leaf_len), f32),
            pltpu.VMEM((points, WIDTH), f32),
            pltpu.VMEM((points, WIDTH), bf16),
            pltpu.VMEM((levels, levels, rhs, rank), f32),
            pltpu.VMEM((levels, levels, rhs, rank), f32),
            pltpu.SemaphoreType.DMA((levels, levels)),
            pltpu.SemaphoreType.DMA((levels, levels)),
            pltpu.SemaphoreType.DMA((leaves,)),
        ],
        compiler_params=params(collective_id=0, has_side_effects=True),
        name="field",
    )(*inputs)
    result = pl.pallas_call(
        place_kernel,
        out_shape=jax.ShapeDtypeStruct((rhs, points), bf16),
        in_specs=[HBM, HBM],
        out_specs=VMEM,
        scratch_shapes=[
            pltpu.SMEM(order.shape, order.dtype),
            pltpu.VMEM((points, WIDTH), bf16),
            pltpu.VMEM((points, WIDTH), f32),
            pltpu.VMEM((points, WIDTH), f32),
            pltpu.SemaphoreType.DMA((5,)),
        ],
        compiler_params=params(),
        name="place",
    )(order, field)
    return result[None, None]


def solution(mesh):
    return jax.shard_map(
        per_device,
        mesh=mesh,
        in_specs=(
            P("top", "leaf", None, None),
            P("top", "leaf", None),
            P("top", "leaf", None, None),
            P("top", "leaf", None, None, None),
            P("top", "leaf", None, None, None, None, None),
            P("top", "leaf", None, None, None),
            P("top", "leaf", None, None, None, None),
        ),
        out_specs=P("top", "leaf", None, None),
        check_vma=False,
    )
```

```python
import functools
import math

import jax
import jax.numpy as jnp
from jax import lax
from jax.experimental import pallas as pl
from jax.experimental.pallas import tpu as pltpu
from jax.sharding import PartitionSpec as P

kernel_rate = 4.0
WIDTH = 128
UNROLL = 32
ROWS = 512
MESH = pl.DeviceIdType.MESH
VMEM = pl.BlockSpec(memory_space=pltpu.VMEM)
HBM = pl.BlockSpec(memory_space=pltpu.HBM)
f32, bf16 = jnp.float32, jnp.bfloat16


def split3(x):
    hi = x.astype(bf16).astype(f32)
    mid = (x - hi).astype(bf16).astype(f32)
    lo = (x - hi - mid).astype(bf16).astype(f32)
    return hi, mid, lo


def dot(a, b, dims=((1,), (0,))):
    return lax.dot_general(a, b, (dims, ((), ())), preferred_element_type=f32)


def dot_split(x, w):
    hi = x.astype(bf16)
    lo = (x - hi.astype(f32)).astype(bf16)
    return dot(hi, w) + dot(lo, w)


def partner(levels_leaf, bits):
    place = {}
    for k in bits:
        axis, bit = ("leaf", k) if k < levels_leaf else ("top", k - levels_leaf)
        me, stride = lax.axis_index(axis), 2**bit
        place[axis] = place.get(axis, me) + stride - 2 * stride * lax.rem(lax.div(me, stride), 2)
    return place


def stages_of(levels):
    stages = []
    for low in range(0, levels, 2):
        stages.append([(low,), (low + 1,), (low, low + 1)] if low + 1 < levels else [(low,)])
    return stages


def takes(bits, level, stage):
    return level >= bits[-1] and not (level == 2 * stage + 1 and bits == (2 * stage,))


def gather_rows(order, coords, charges, rows, src, dst):
    rhs, points = charges.shape
    dim = coords.shape[0]
    step = 512
    scale = (2.0 * kernel_rate / math.log(2.0)) ** 0.5
    for start in range(0, points, step):
        cols = pl.ds(start, step)
        pts = coords[:, cols] * scale
        hi, mid, lo = split3(pts)
        n_hi, n_mid, n_lo = split3(-0.5 * jnp.sum(pts * pts, axis=0, keepdims=True))
        left = WIDTH - rhs - 6 * dim
        row = lax.broadcasted_iota(jnp.int32, (left, step), 0)
        tail = jnp.where(row < 6, 1.0, 0.0)
        tail = jnp.where(row == 0, n_hi, jnp.where(row == 1, n_mid, jnp.where(row == 2, n_lo, tail)))
        whole = jnp.concatenate([charges[:, cols].astype(f32), hi, hi, mid, hi, lo, mid, tail], axis=0)
        src[cols, :] = whole.T

    @pl.loop(0, points // UNROLL)
    def _(block):
        base = pl.multiple_of(block * UNROLL, UNROLL)
        got = [src[pl.ds(order[base + u], 1), :] for u in range(UNROLL)]
        for u in range(UNROLL):
            dst[pl.ds(base + u, 1), :] = got[u]

    rows[...] = dst[...].astype(bf16)


def field_kernel(levels_leaf, *refs):
    given, field, held_in, in_sems = refs[:7], refs[7], refs[8:15], refs[15]
    order, coords, charges, basis, leaf_factors, transfer, factors = held_in
    src, dst, rows, skel, terms, right, basis_t, local, power, out, stage, got, held, send, recv, out_sems = refs[16:]
    levels, rhs, rank = terms.shape
    leaves, _, leaf_len = basis.shape
    inputs = [pltpu.make_async_copy(a, b, in_sems.at[i]) for i, (a, b) in enumerate(zip(given, held_in))]
    for i in (1, 2, 0, 3, 5, 6, 4):
        inputs[i].start()
    barrier = pltpu.get_barrier_semaphore()
    stages = stages_of(levels)
    others = [bits for stage in stages for bits in stage]
    for bits in others:
        pl.semaphore_signal(barrier, inc=1, device_id=partner(levels_leaf, bits), device_id_type=MESH)
    for i in (1, 2, 0):
        inputs[i].wait()
    gather_rows(order, coords, charges, rows, src, dst)
    for i in (3, 5, 6):
        inputs[i].wait()
    total = jnp.zeros((rhs, rank), f32)
    for j in range(leaves):
        mine = dot(basis[j], rows[pl.ds(j * leaf_len, leaf_len), :]).T[:rhs]
        skel[j] = mine
        total = total + dot_split(mine, transfer[j])
    for k in range(levels):
        terms[k] = dot_split(total, factors[k, 0])
    pl.semaphore_wait(barrier, len(others))

    copies = {}

    def start(stage, level):
        for i, bits in enumerate(stages[stage]):
            if takes(bits, level, stage):
                copies[stage, i, level] = pltpu.make_async_remote_copy(
                    src_ref=terms.at[level] if stage == 0 else held.at[stage, level],
                    dst_ref=got.at[stage, i, level],
                    send_sem=send.at[stage, i, level],
                    recv_sem=recv.at[stage, i, level],
                    device_id=partner(levels_leaf, bits),
                    device_id_type=MESH,
                )
                copies[stage, i, level].start()

    for level in reversed(range(levels)):
        start(0, level)

    coeffs = [jnp.zeros((rhs, rank), f32)]

    def receive(stage, level):
        heard = None
        for i, bits in enumerate(stages[stage]):
            if takes(bits, level, stage):
                copies[stage, i, level].wait_recv()
                part = got[stage, i, level]
                heard = part if heard is None else heard + part
        if level <= 2 * stage + 1:
            coeffs[0] = coeffs[0] + dot_split(heard * 0.5 ** (level / 2.0), factors[level, 1])
        else:
            held[stage + 1, level] = (terms[level] if stage == 0 else held[stage, level]) + heard
            start(stage + 1, level)

    def right_rows(j):
        lane = lax.broadcasted_iota(jnp.int32, (WIDTH, WIDTH), 0)
        lane_in = lax.broadcasted_iota(jnp.int32, (WIDTH, WIDTH), 1)
        dim = 8
        tail = rhs + 6 * dim
        source = lane
        for slot, shift in ((1, dim), (2, -2 * dim), (3, dim), (4, -4 * dim)):
            low = rhs + slot * dim
            source = jnp.where((lane >= low) & (lane < low + dim), lane + shift, source)
        source = jnp.where((lane >= tail) & (lane < tail + 3), lane + 3, source)
        source = jnp.where((lane >= tail + 3) & (lane < tail + 6), lane - 3, source)
        source = jnp.where((lane < rhs) | (lane >= tail + 6), -1, source)
        chosen = jnp.where(lane_in == source, 1.0, 0.0).astype(bf16)
        right[j] = dot(chosen, rows[pl.ds(j * leaf_len, leaf_len), :], ((1,), (1,))).astype(bf16)

    def turn_basis(j):
        basis_t[j] = basis[j].T

    blocks = [(j, start_row) for j in range(leaves) for start_row in range(0, leaf_len, ROWS)]

    def exponent(i):
        j, start_row = blocks[i]
        power[i % 2] = dot(rows[pl.ds(j * leaf_len + start_row, ROWS), :], right[j])

    def near(i):
        j, start_row = blocks[i]
        if i + 1 < len(blocks):
            exponent(i + 1)
        values = jnp.exp2(power[i % 2]).astype(bf16)
        out[pl.ds(j * leaf_len + start_row, ROWS), :] = dot(values, rows[pl.ds(j * leaf_len, leaf_len), :])

    def local_terms(h):
        width = 2**h
        part = [dot_split(skel[j], leaf_factors[j, h, 0]) for j in range(leaves)]
        for j in range(leaves):
            other = (j // width ^ 1) * width
            summed = part[other]
            for i in range(1, width):
                summed = summed + part[other + i]
            mine = dot_split(summed * 0.5 ** (h / 2.0), leaf_factors[j, h, 1])
            local[j] = mine if h == 0 else local[j] + mine

    tasks = [functools.partial(right_rows, j) for j in range(leaves)]
    tasks += [functools.partial(turn_basis, j) for j in range(leaves)]
    tasks += [inputs[4].wait]
    tasks += [functools.partial(local_terms, h) for h in range(leaf_factors.shape[1])]
    tasks += [functools.partial(exponent, 0)]
    first = len(tasks)
    tasks += [functools.partial(near, i) for i in range(len(blocks))]
    events = [(t, level) for t in range(len(stages)) for level in range(2 * t, levels)]
    events.sort(key=lambda event: (2 * event[0] + levels - 1 - event[1], event[0]))
    done = 0
    for i, task in enumerate(tasks):
        task()
        while done < min(len(events), len(events) * (i + 1 - first) // (len(tasks) - first - 1)):
            receive(*events[done])
            done += 1
    for copy in copies.values():
        copy.wait_send()

    none = jnp.zeros((WIDTH - rhs, rank), f32)
    whole = jnp.concatenate([coeffs[0], none], axis=0).T
    hi = whole.astype(bf16)
    lo = (whole - hi.astype(f32)).astype(bf16)
    leaving = []
    for j in range(leaves):
        span = pl.ds(j * leaf_len, leaf_len)
        own = jnp.concatenate([local[j], none], axis=0).T
        mine = (dot(transfer[j], hi) + dot(transfer[j], lo) + own).astype(bf16)
        stage[span, :] = (out[span, :] + dot(basis_t[j], mine)).astype(bf16)
        leaving.append(pltpu.make_async_copy(stage.at[span, :], field.at[span, :], out_sems.at[j]))
        leaving[j].start()
    for copy in leaving:
        copy.wait()


def place_kernel(order_in, field_in, out, order, field, src, dst, sems):
    rhs, points = out.shape
    pieces = 4
    size = points // pieces
    copies = [pltpu.make_async_copy(order_in, order, sems.at[pieces])]
    for i in range(pieces):
        span = pl.ds(i * size, size)
        copies.append(pltpu.make_async_copy(field_in.at[span, :], field.at[span, :], sems.at[i]))
    for copy in copies:
        copy.start()
    copies[0].wait()
    for i in range(pieces):
        copies[i + 1].wait()
        span = pl.ds(i * size, size)
        src[span, :] = field[span, :].astype(f32)

        @pl.loop(0, size // UNROLL)
        def _(block):
            base = pl.multiple_of(i * size + block * UNROLL, UNROLL)
            got = [src[pl.ds(base + u, 1), :] for u in range(UNROLL)]
            for u in range(UNROLL):
                dst[pl.ds(order[base + u], 1), :] = got[u]

    step = 512
    for start in range(0, points, step):
        out[:, pl.ds(start, step)] = dst[pl.ds(start, step), :].T[:rhs].astype(bf16)


def params(**more):
    return pltpu.CompilerParams(vmem_limit_bytes=60 * 2**20, **more)


def per_device(coords, order, charges, leaf_basis, leaf_factors, transfer, block_factors):
    coords, order, charges, basis = coords[0, 0], order[0, 0], charges[0, 0], leaf_basis[0, 0]
    leaf_factors, transfer, factors = leaf_factors[0, 0], transfer[0, 0], block_factors[0, 0]
    rhs, points = charges.shape
    leaves, rank, leaf_len = basis.shape
    levels = factors.shape[0]
    levels_leaf = lax.axis_size("leaf").bit_length() - 1
    stages = len(stages_of(levels))
    inputs = (order, coords, charges, basis, leaf_factors, transfer, factors)
    in_vmem = [pltpu.VMEM(a.shape, a.dtype) for a in inputs[1:]]
    field = pl.pallas_call(
        functools.partial(field_kernel, levels_leaf),
        out_shape=jax.ShapeDtypeStruct((points, WIDTH), bf16),
        in_specs=[HBM] * len(inputs),
        out_specs=HBM,
        scratch_shapes=[
            pltpu.SMEM(order.shape, order.dtype),
            *in_vmem,
            pltpu.SemaphoreType.DMA((len(inputs),)),
            pltpu.VMEM((points, WIDTH), f32),
            pltpu.VMEM((points, WIDTH), f32),
            pltpu.VMEM((points, WIDTH), bf16),
            pltpu.VMEM((leaves, rhs, rank), f32),
            pltpu.VMEM((levels, rhs, rank), f32),
            pltpu.VMEM((leaves, WIDTH, leaf_len), bf16),
            pltpu.VMEM((leaves, leaf_len, rank), bf16),
            pltpu.VMEM((leaves, rhs, rank), f32),
            pltpu.VMEM((2, ROWS, leaf_len), f32),
            pltpu.VMEM((points, WIDTH), f32),
            pltpu.VMEM((points, WIDTH), bf16),
            pltpu.VMEM((stages, 3, levels, rhs, rank), f32),
            pltpu.VMEM((stages, levels, rhs, rank), f32),
            pltpu.SemaphoreType.DMA((stages, 3, levels)),
            pltpu.SemaphoreType.DMA((stages, 3, levels)),
            pltpu.SemaphoreType.DMA((leaves,)),
        ],
        compiler_params=params(collective_id=0, has_side_effects=True),
        name="field",
    )(*inputs)
    result = pl.pallas_call(
        place_kernel,
        out_shape=jax.ShapeDtypeStruct((rhs, points), bf16),
        in_specs=[HBM, HBM],
        out_specs=VMEM,
        scratch_shapes=[
            pltpu.SMEM(order.shape, order.dtype),
            pltpu.VMEM((points, WIDTH), bf16),
            pltpu.VMEM((points, WIDTH), f32),
            pltpu.VMEM((points, WIDTH), f32),
            pltpu.SemaphoreType.DMA((5,)),
        ],
        compiler_params=params(),
        name="place",
    )(order, field)
    return result[None, None]


def solution(mesh):
    return jax.shard_map(
        per_device,
        mesh=mesh,
        in_specs=(
            P("top", "leaf", None, None),
            P("top", "leaf", None),
            P("top", "leaf", None, None),
            P("top", "leaf", None, None, None),
            P("top", "leaf", None, None, None, None, None),
            P("top", "leaf", None, None, None),
            P("top", "leaf", None, None, None, None),
        ),
        out_specs=P("top", "leaf", None, None),
        check_vma=False,
    )
```

```python
import functools
import math

import jax
import jax.numpy as jnp
from jax import lax
from jax.experimental import pallas as pl
from jax.experimental.pallas import tpu as pltpu
from jax.sharding import PartitionSpec as P

kernel_rate = 4.0
WIDTH = 128
UNROLL = 32
ROWS = 512
MESH = pl.DeviceIdType.MESH
VMEM = pl.BlockSpec(memory_space=pltpu.VMEM)
HBM = pl.BlockSpec(memory_space=pltpu.HBM)
f32, bf16 = jnp.float32, jnp.bfloat16


def split3(x):
    hi = x.astype(bf16).astype(f32)
    mid = (x - hi).astype(bf16).astype(f32)
    lo = (x - hi - mid).astype(bf16).astype(f32)
    return hi, mid, lo


def dot(a, b, dims=((1,), (0,))):
    return lax.dot_general(a, b, (dims, ((), ())), preferred_element_type=f32)


def dot_split(x, w):
    hi = x.astype(bf16)
    lo = (x - hi.astype(f32)).astype(bf16)
    return dot(hi, w) + dot(lo, w)


def partner(levels_leaf, bits):
    place = {}
    for k in bits:
        axis, bit = ("leaf", k) if k < levels_leaf else ("top", k - levels_leaf)
        me, stride = lax.axis_index(axis), 2**bit
        place[axis] = place.get(axis, me) + stride - 2 * stride * lax.rem(lax.div(me, stride), 2)
    return place


def stages_of(levels):
    stages = []
    for low in range(0, levels, 2):
        stages.append([(low,), (low + 1,), (low, low + 1)] if low + 1 < levels else [(low,)])
    return stages


def takes(bits, level, stage):
    return level >= bits[-1] and not (level == 2 * stage + 1 and bits == (2 * stage,))


def gather_rows(order, coords, charges, rows, src, dst):
    rhs, points = charges.shape
    dim = coords.shape[0]
    step = 512
    scale = (2.0 * kernel_rate / math.log(2.0)) ** 0.5
    for start in range(0, points, step):
        cols = pl.ds(start, step)
        pts = coords[:, cols] * scale
        hi, mid, lo = split3(pts)
        n_hi, n_mid, n_lo = split3(-0.5 * jnp.sum(pts * pts, axis=0, keepdims=True))
        left = WIDTH - rhs - 6 * dim
        row = lax.broadcasted_iota(jnp.int32, (left, step), 0)
        tail = jnp.where(row < 6, 1.0, 0.0)
        tail = jnp.where(row == 0, n_hi, jnp.where(row == 1, n_mid, jnp.where(row == 2, n_lo, tail)))
        whole = jnp.concatenate([charges[:, cols].astype(f32), hi, hi, mid, hi, lo, mid, tail], axis=0)
        src[cols, :] = whole.T

    @pl.loop(0, points // UNROLL)
    def _(block):
        base = pl.multiple_of(block * UNROLL, UNROLL)
        got = [src[pl.ds(order[base + u], 1), :] for u in range(UNROLL)]
        for u in range(UNROLL):
            dst[pl.ds(base + u, 1), :] = got[u]

    rows[...] = dst[...].astype(bf16)


def field_kernel(levels_leaf, *refs):
    given, field, held_in, in_sems = refs[:7], refs[7], refs[8:15], refs[15]
    order, coords, charges, basis, leaf_factors, transfer, factors = held_in
    src, dst, rows, skel, terms, right, basis_t, local, power, out, stage, got, held, send, recv, out_sems = refs[16:]
    levels, rhs, rank = terms.shape
    leaves, _, leaf_len = basis.shape
    inputs = [pltpu.make_async_copy(a, b, in_sems.at[i]) for i, (a, b) in enumerate(zip(given, held_in))]
    for i in (1, 2, 0, 3, 5, 6, 4):
        inputs[i].start()
    barrier = pltpu.get_barrier_semaphore()
    stages = stages_of(levels)
    others = [bits for stage in stages for bits in stage]
    for bits in others:
        pl.semaphore_signal(barrier, inc=1, device_id=partner(levels_leaf, bits), device_id_type=MESH)
    for i in (1, 2, 0):
        inputs[i].wait()
    gather_rows(order, coords, charges, rows, src, dst)
    for i in (3, 5, 6):
        inputs[i].wait()
    total = jnp.zeros((rhs, rank), f32)
    for j in range(leaves):
        mine = dot(basis[j], rows[pl.ds(j * leaf_len, leaf_len), :]).T[:rhs]
        skel[j] = mine
        total = total + dot_split(mine, transfer[j])
    for k in range(levels):
        terms[k] = dot_split(total, factors[k, 0])
    pl.semaphore_wait(barrier, len(others))

    copies = {}

    def start(stage, level):
        for i, bits in enumerate(stages[stage]):
            if takes(bits, level, stage):
                copies[stage, i, level] = pltpu.make_async_remote_copy(
                    src_ref=terms.at[level] if stage == 0 else held.at[stage, level],
                    dst_ref=got.at[stage, i, level],
                    send_sem=send.at[stage, i, level],
                    recv_sem=recv.at[stage, i, level],
                    device_id=partner(levels_leaf, bits),
                    device_id_type=MESH,
                )
                copies[stage, i, level].start()

    for level in reversed(range(levels)):
        start(0, level)

    coeffs = [jnp.zeros((rhs, rank), f32)]

    def receive(stage, level):
        heard = None
        for i, bits in enumerate(stages[stage]):
            if takes(bits, level, stage):
                copies[stage, i, level].wait_recv()
                part = got[stage, i, level]
                heard = part if heard is None else heard + part
        if level <= 2 * stage + 1:
            coeffs[0] = coeffs[0] + dot_split(heard * 0.5 ** (level / 2.0), factors[level, 1])
        else:
            held[stage + 1, level] = (terms[level] if stage == 0 else held[stage, level]) + heard
            start(stage + 1, level)

    def right_rows(j):
        lane = lax.broadcasted_iota(jnp.int32, (WIDTH, WIDTH), 0)
        lane_in = lax.broadcasted_iota(jnp.int32, (WIDTH, WIDTH), 1)
        dim = 8
        tail = rhs + 6 * dim
        source = lane
        for slot, shift in ((1, dim), (2, -2 * dim), (3, dim), (4, -4 * dim)):
            low = rhs + slot * dim
            source = jnp.where((lane >= low) & (lane < low + dim), lane + shift, source)
        source = jnp.where((lane >= tail) & (lane < tail + 3), lane + 3, source)
        source = jnp.where((lane >= tail + 3) & (lane < tail + 6), lane - 3, source)
        source = jnp.where((lane < rhs) | (lane >= tail + 6), -1, source)
        chosen = jnp.where(lane_in == source, 1.0, 0.0).astype(bf16)
        right[j] = dot(chosen, rows[pl.ds(j * leaf_len, leaf_len), :], ((1,), (1,))).astype(bf16)

    def turn_basis(j):
        basis_t[j] = basis[j].T

    blocks = [(j, start_row) for j in range(leaves) for start_row in range(0, leaf_len, ROWS)]

    def exponent(i):
        j, start_row = blocks[i]
        power[i % 2] = dot(rows[pl.ds(j * leaf_len + start_row, ROWS), :], right[j])

    def near(i):
        j, start_row = blocks[i]
        if i + 1 < len(blocks):
            exponent(i + 1)
        values = jnp.exp2(power[i % 2]).astype(bf16)
        out[pl.ds(j * leaf_len + start_row, ROWS), :] = dot(values, rows[pl.ds(j * leaf_len, leaf_len), :])

    def local_terms(h):
        width = 2**h
        part = [dot_split(skel[j], leaf_factors[j, h, 0]) for j in range(leaves)]
        for j in range(leaves):
            other = (j // width ^ 1) * width
            summed = part[other]
            for i in range(1, width):
                summed = summed + part[other + i]
            mine = dot_split(summed * 0.5 ** (h / 2.0), leaf_factors[j, h, 1])
            local[j] = mine if h == 0 else local[j] + mine

    tasks = [functools.partial(right_rows, j) for j in range(leaves)]
    tasks += [functools.partial(turn_basis, j) for j in range(leaves)]
    tasks += [inputs[4].wait]
    tasks += [functools.partial(local_terms, h) for h in range(leaf_factors.shape[1])]
    tasks += [functools.partial(exponent, 0)]
    first = len(tasks)
    tasks += [functools.partial(near, i) for i in range(len(blocks))]
    events = [(t, level) for t in range(len(stages)) for level in range(2 * t, levels)]
    events.sort(key=lambda event: (2 * event[0] + levels - 1 - event[1], event[0]))
    done = 0
    for i, task in enumerate(tasks):
        task()
        while done < min(len(events), len(events) * (i + 1 - first) // (len(tasks) - first - 1)):
            receive(*events[done])
            done += 1
    for copy in copies.values():
        copy.wait_send()

    none = jnp.zeros((WIDTH - rhs, rank), f32)
    whole = jnp.concatenate([coeffs[0], none], axis=0).T
    hi = whole.astype(bf16)
    lo = (whole - hi.astype(f32)).astype(bf16)
    leaving = []
    for j in range(leaves):
        span = pl.ds(j * leaf_len, leaf_len)
        own = jnp.concatenate([local[j], none], axis=0).T
        mine = (dot(transfer[j], hi) + dot(transfer[j], lo) + own).astype(bf16)
        stage[span, :] = (out[span, :] + dot(basis_t[j], mine)).astype(bf16)
        leaving.append(pltpu.make_async_copy(stage.at[span, :], field.at[span, :], out_sems.at[j]))
        leaving[j].start()
    for copy in leaving:
        copy.wait()


def place_kernel(order_in, field_in, out, order, field, src, dst, turned, sems, out_sems):
    rhs, points = out.shape
    pieces = 4
    size = points // pieces
    copies = [pltpu.make_async_copy(order_in, order, sems.at[pieces])]
    for i in range(pieces):
        span = pl.ds(i * size, size)
        copies.append(pltpu.make_async_copy(field_in.at[span, :], field.at[span, :], sems.at[i]))
    for copy in copies:
        copy.start()
    copies[0].wait()
    for i in range(pieces):
        copies[i + 1].wait()
        span = pl.ds(i * size, size)
        src[span, :] = field[span, :].astype(f32)

        @pl.loop(0, size // UNROLL)
        def _(block):
            base = pl.multiple_of(i * size + block * UNROLL, UNROLL)
            got = [src[pl.ds(base + u, 1), :] for u in range(UNROLL)]
            for u in range(UNROLL):
                dst[pl.ds(order[base + u], 1), :] = got[u]

    step = points // 4
    leaving = []
    for i in range(4):
        span = pl.ds(i * step, step)
        turned[:, span] = dst[span, :].astype(bf16).T[:rhs]
        leaving.append(pltpu.make_async_copy(turned.at[:, span], out.at[:, span], out_sems.at[i]))
        leaving[i].start()
    for copy in leaving:
        copy.wait()


def params(**more):
    return pltpu.CompilerParams(vmem_limit_bytes=60 * 2**20, **more)


def per_device(coords, order, charges, leaf_basis, leaf_factors, transfer, block_factors):
    coords, order, charges, basis = coords[0, 0], order[0, 0], charges[0, 0], leaf_basis[0, 0]
    leaf_factors, transfer, factors = leaf_factors[0, 0], transfer[0, 0], block_factors[0, 0]
    rhs, points = charges.shape
    leaves, rank, leaf_len = basis.shape
    levels = factors.shape[0]
    levels_leaf = lax.axis_size("leaf").bit_length() - 1
    stages = len(stages_of(levels))
    inputs = (order, coords, charges, basis, leaf_factors, transfer, factors)
    in_vmem = [pltpu.VMEM(a.shape, a.dtype) for a in inputs[1:]]
    field = pl.pallas_call(
        functools.partial(field_kernel, levels_leaf),
        out_shape=jax.ShapeDtypeStruct((points, WIDTH), bf16),
        in_specs=[HBM] * len(inputs),
        out_specs=HBM,
        scratch_shapes=[
            pltpu.SMEM(order.shape, order.dtype),
            *in_vmem,
            pltpu.SemaphoreType.DMA((len(inputs),)),
            pltpu.VMEM((points, WIDTH), f32),
            pltpu.VMEM((points, WIDTH), f32),
            pltpu.VMEM((points, WIDTH), bf16),
            pltpu.VMEM((leaves, rhs, rank), f32),
            pltpu.VMEM((levels, rhs, rank), f32),
            pltpu.VMEM((leaves, WIDTH, leaf_len), bf16),
            pltpu.VMEM((leaves, leaf_len, rank), bf16),
            pltpu.VMEM((leaves, rhs, rank), f32),
            pltpu.VMEM((2, ROWS, leaf_len), f32),
            pltpu.VMEM((points, WIDTH), f32),
            pltpu.VMEM((points, WIDTH), bf16),
            pltpu.VMEM((stages, 3, levels, rhs, rank), f32),
            pltpu.VMEM((stages, levels, rhs, rank), f32),
            pltpu.SemaphoreType.DMA((stages, 3, levels)),
            pltpu.SemaphoreType.DMA((stages, 3, levels)),
            pltpu.SemaphoreType.DMA((leaves,)),
        ],
        compiler_params=params(collective_id=0, has_side_effects=True),
        name="field",
    )(*inputs)
    result = pl.pallas_call(
        place_kernel,
        out_shape=jax.ShapeDtypeStruct((rhs, points), bf16),
        in_specs=[HBM, HBM],
        out_specs=HBM,
        scratch_shapes=[
            pltpu.SMEM(order.shape, order.dtype),
            pltpu.VMEM((points, WIDTH), bf16),
            pltpu.VMEM((points, WIDTH), f32),
            pltpu.VMEM((points, WIDTH), f32),
            pltpu.VMEM((rhs, points), bf16),
            pltpu.SemaphoreType.DMA((5,)),
            pltpu.SemaphoreType.DMA((4,)),
        ],
        compiler_params=params(),
        name="place",
    )(order, field)
    return result[None, None]


def solution(mesh):
    return jax.shard_map(
        per_device,
        mesh=mesh,
        in_specs=(
            P("top", "leaf", None, None),
            P("top", "leaf", None),
            P("top", "leaf", None, None),
            P("top", "leaf", None, None, None),
            P("top", "leaf", None, None, None, None, None),
            P("top", "leaf", None, None, None),
            P("top", "leaf", None, None, None, None),
        ),
        out_specs=P("top", "leaf", None, None),
        check_vma=False,
    )
```
